32 devices in a mesh: dp: 8 (over z, x), tensor: 4 (over y, core).
Axes of the slice: x: 2, y: 2, z: 4, core: 2. Of those that a mesh axis runs over, the one named last changes fastest.
Arguments:
- tokens: bfloat16 [8192, 1024], P(('dp', 'tensor')), may hold values from -6 to 6
- cotangent: bfloat16 [8192, 1024], P(('dp', 'tensor')), may hold values from -6 to 6
- seq_lengths: int32 [8, 8], P('dp'), may hold values from 0 to 1024, as said below
- ln1_gain: bfloat16 [1024], replicated, may hold values from 0.099609375 to 1.8984375
- ln1_bias: bfloat16 [1024], replicated, may hold values from -3 to 3
- qkv_weight: bfloat16 [1024, 3072], P(None, 'tensor'), may hold values from -0.1875 to 0.1875
- qv_bias: bfloat16 [2048], P('tensor'), may hold values from -3 to 3
- dense_weight: bfloat16 [1024, 1024], P('tensor'), may hold values from -0.75 to 0.75
- dense_bias: bfloat16 [1024], replicated, may hold values from -3 to 3
- ln2_gain: bfloat16 [1024], replicated, may hold values from 0.099609375 to 1.8984375
- ln2_bias: bfloat16 [1024], replicated, may hold values from -3 to 3
- up_weight: bfloat16 [1024, 4096], P(None, 'tensor'), may hold values from -0.1875 to 0.1875
- up_bias: bfloat16 [4096], P('tensor'), may hold values from -3 to 3
- down_weight: bfloat16 [4096, 1024], P('tensor'), may hold values from -0.09375 to 0.09375
- down_bias: bfloat16 [1024], replicated, may hold values from -3 to 3
Outputs:
- output: bfloat16 [8192, 1024], P(('dp', 'tensor'))
- grad_tokens: bfloat16 [8192, 1024], P(('dp', 'tensor'))
- grad_ln1_gain: float32 [1024], replicated
- grad_ln1_bias: float32 [1024], replicated
- grad_qkv_weight: float32 [1024, 3072], P(None, 'tensor')
- grad_qv_bias: float32 [2048], P('tensor')
- grad_dense_weight: float32 [1024, 1024], P('tensor')
- grad_dense_bias: float32 [1024], replicated
- grad_ln2_gain: float32 [1024], replicated
- grad_ln2_bias: float32 [1024], replicated
- grad_up_weight: float32 [1024, 4096], P(None, 'tensor')
- grad_up_bias: float32 [4096], P('tensor')
- grad_down_weight: float32 [4096, 1024], P('tensor')
- grad_down_bias: float32 [1024], replicated
The draws below stay inside these ranges and needn't reach their ends.
Inputs may be any that keep to these rules, and one draw needn't show every extreme that they name: `seq_lengths`: each row sums to 1024; entries of 0 are empty sequences and may stand anywhere in a row; in every draw some row holds one sequence of all 1024 tokens.
All inputs are finite; a program needn't handle non-finite values.
Results may differ from the reference program's by a relative error of at most 0.018.
Values may be sent and summed in bfloat16 or wider, within the bound.
No kernel may reach another device: no remote copies, remote signals or barrier semaphores. Data moves between devices by JAX's collectives and lax.ppermute only.
A program may use at most 128 MiB of HBM per device.

```python
import math
import jax
import jax.numpy as jnp
from jax import lax

D = 1024
H = 16
HEAD = 64
FF = 4096
TOK_DEV = 1024
SEGS = 8
SHARDS = 8
TOKENS = 8192


def draw_seq_lengths(key, part):
    key = jax.random.fold_in(key, 11)
    key_counts, key_cuts, key_whole = jax.random.split(key, 3)
    counts = jax.random.randint(key_counts, (SHARDS,), 1, SEGS + 1)
    whole = jax.random.randint(key_whole, (), 0, SHARDS)
    counts = jnp.where(jnp.arange(SHARDS) == whole, 1, counts)
    cuts = jax.random.randint(key_cuts, (SHARDS, SEGS - 1), 1, TOK_DEV)
    used = jnp.arange(SEGS - 1)[None, :] < counts[:, None] - 1
    cuts = jnp.sort(jnp.where(used, cuts, TOK_DEV), axis=1)
    edges = jnp.concatenate([jnp.zeros((SHARDS, 1), jnp.int32), cuts.astype(jnp.int32), jnp.full((SHARDS, 1), TOK_DEV, jnp.int32)], axis=1)
    return (edges[:, 1:] - edges[:, :-1]).astype(jnp.int32)


def shard_levels(stream_key, shape, cuts, least, top_value):
    level = 1.0
    for position, parts in cuts:
        steps = jax.random.uniform(jax.random.fold_in(jax.random.fold_in(stream_key, 6), position), (parts,), jnp.float32, least / len(cuts), top_value / len(cuts))
        level = level * jnp.repeat(jnp.exp(steps), shape[position] // parts).reshape((-1,) + (1,) * (len(shape) - 1 - position))
    return level


def normal_values(stream_key, shape, scale, reach, cuts=(), held_as=jnp.bfloat16):
    values = scale * jax.random.normal(stream_key, shape, jnp.float32)
    if cuts:
        values = values * shard_levels(stream_key, shape, cuts, -0.22, 0.18)
    return jnp.clip(values, -reach, reach).astype(held_as)


def setup_inputs(seed: int = 0) -> dict:
    splits = jax.random.split(jax.random.key(seed), 16)
    tokens = normal_values(splits[0], (TOKENS, D), 1.0, 6.0, ((0, 32),))
    cotangent = normal_values(splits[1], (TOKENS, D), 1.0, 6.0, ((0, 32),))
    seq_lengths = draw_seq_lengths(jax.random.fold_in(splits[15], 71), 0)
    ln1_gain = jnp.clip(1.0 + 0.18 * jax.random.normal(splits[3], (D,), jnp.float32), 0.099609375, 1.8984375).astype(jnp.bfloat16)
    ln1_bias = normal_values(splits[4], (D,), 0.5, 3.0)
    qkv_weight = normal_values(splits[5], (D, 3 * D), D ** -0.5, 0.1875, ((1, 4),))
    qv_bias = normal_values(splits[6], (2 * D,), 0.5, 3.0, ((0, 4),))
    dense_weight = normal_values(splits[7], (D, D), HEAD ** -0.5, 0.75, ((0, 4),))
    dense_bias = normal_values(splits[8], (D,), 0.5, 3.0)
    ln2_gain = jnp.clip(1.0 + 0.18 * jax.random.normal(splits[9], (D,), jnp.float32), 0.099609375, 1.8984375).astype(jnp.bfloat16)
    ln2_bias = normal_values(splits[10], (D,), 0.5, 3.0)
    up_weight = normal_values(splits[11], (D, FF), D ** -0.5, 0.1875, ((1, 4),))
    up_bias = normal_values(splits[12], (FF,), 0.5, 3.0, ((0, 4),))
    down_weight = normal_values(splits[13], (FF, D), FF ** -0.5, 0.09375, ((0, 4),))
    down_bias = normal_values(splits[14], (D,), 0.5, 3.0)
    return {"tokens": tokens, "cotangent": cotangent, "seq_lengths": seq_lengths, "ln1_gain": ln1_gain, "ln1_bias": ln1_bias, "qkv_weight": qkv_weight, "qv_bias": qv_bias, "dense_weight": dense_weight, "dense_bias": dense_bias, "ln2_gain": ln2_gain, "ln2_bias": ln2_bias, "up_weight": up_weight, "up_bias": up_bias, "down_weight": down_weight, "down_bias": down_bias}


EPS = 1e-05
NEG = -1e+30

@jax.custom_vjp
def low(v):
    return lax.optimization_barrier(v.astype(jnp.bfloat16)).astype(jnp.float32)

@jax.custom_vjp
def low_back(v):
    return v

def low_keep(v):
    return (low(v), None)

def low_pass(kept, grad):
    return (grad,)

def back_keep(v):
    return (v, None)

def back_low(kept, grad):
    return (low(grad),)
low.defvjp(low_keep, low_pass)
low_back.defvjp(back_keep, back_low)

def product(left, right):
    return jnp.dot(left, right, precision=lax.Precision.HIGHEST)

def layer_norm(values, gain, shift):
    mean = lax.optimization_barrier(jnp.mean(values, axis=-1, keepdims=True))
    centred = values - mean
    spread = lax.optimization_barrier(jnp.mean(centred * centred, axis=-1, keepdims=True))
    return centred * lax.rsqrt(spread + EPS) * gain + shift

def reference(tokens, cotangent, seq_lengths, ln1_gain, ln1_bias, qkv_weight, qv_bias, dense_weight, dense_bias, ln2_gain, ln2_bias, up_weight, up_bias, down_weight, down_bias):
    scale = 1.0 / math.sqrt(HEAD)
    index = jnp.arange(TOK_DEV, dtype=jnp.int32)
    ends = jnp.cumsum(seq_lengths, axis=1)
    segment = lax.optimization_barrier(jnp.sum((ends[:, None, :] <= index[None, :, None]).astype(jnp.int32), axis=2)).astype(jnp.int32)
    heads = jnp.arange(H).astype(jnp.float32)
    slopes = jnp.exp2(-8.0 * (heads + 1.0) / H)

    def attend_shard(item):
        grouped, seg_row = item
        distance = (index[:, None] - index[None, :]).astype(jnp.float32)
        allowed = (seg_row[:, None] == seg_row[None, :]) & (distance >= 0.0)

        def attend_head(head_item):
            query, keys, values, slope = head_item
            scores = product(query, keys.T) * scale - slope * distance
            scores = low_back(scores)
            scores = jnp.where(allowed, scores, NEG)
            probs = jax.nn.softmax(scores, axis=-1)
            return product(low(probs), values)
        return lax.map(jax.checkpoint(attend_head), (grouped[0], grouped[1], grouped[2], slopes))

    def forward(x, gain1, shift1, w_qkv, b_qv, w_dense, b_dense, gain2, shift2, w_up, b_up, w_down, b_down):
        normed1 = low(layer_norm(x, gain1, shift1))
        pair = b_qv.reshape(H, 2, HEAD)
        bias_full = jnp.stack([pair[:, 0], jnp.zeros_like(pair[:, 0]), pair[:, 1]], axis=1).reshape(3 * D)
        qkv = low(low_back(product(normed1, w_qkv) + bias_full))
        grouped = qkv.reshape(SHARDS, TOK_DEV, H, 3, HEAD).transpose(0, 3, 2, 1, 4)
        context = lax.map(jax.checkpoint(attend_shard), (grouped, segment))
        context = context.transpose(0, 2, 1, 3).reshape(TOKENS, D)
        context = low(low_back(context))
        resid = x + low_back(product(context, w_dense) + b_dense)
        normed2 = low(layer_norm(resid, gain2, shift2))
        hidden_pre = low_back(product(normed2, w_up) + b_up)
        activated = low(jax.nn.gelu(hidden_pre, approximate=True))
        return resid + product(activated, w_down) + b_down
    floats = [a.astype(jnp.float32) for a in (tokens, ln1_gain, ln1_bias, qkv_weight, qv_bias, dense_weight, dense_bias, ln2_gain, ln2_bias, up_weight, up_bias, down_weight, down_bias)]
    output, pullback = jax.vjp(forward, *floats)
    grads = pullback(cotangent.astype(jnp.float32))
    return (output.astype(jnp.bfloat16), grads[0].astype(jnp.bfloat16), grads[1], grads[2], grads[3], grads[4], grads[5], grads[6], grads[7], grads[8], grads[9], grads[10], grads[11], grads[12])
```

```python
import math

import jax
import jax.numpy as jnp
from jax import lax
from jax.experimental import pallas as pl
from jax.experimental.pallas import tpu as pltpu
from jax.sharding import PartitionSpec as P

H = 16
HEAD = 64
EPS = 1e-05
FAR = 1e34
BF = jnp.bfloat16
F32 = jnp.float32
SCALE = 1.0 / math.sqrt(HEAD)
TENSOR = 4
VMEM_LIMIT = 40 * 1024 * 1024


def dot(left, right, left_dim=1, right_dim=0):
    return lax.dot_general(
        left, right, (((left_dim,), (right_dim,)), ((), ())), preferred_element_type=F32
    )


def after(values, *earlier):
    return lax.optimization_barrier((values,) + earlier)[0]


def swap(value, mask):
    return lax.ppermute(value, "tensor", [(i, i ^ mask) for i in range(TENSOR)])


def gather(block):
    across = swap(block, 2)
    beside = swap(block, 1)
    return [block, across, beside, swap(across, 1)]


def scatter_sum(keep, send):
    half = keep.shape[0] // 2
    got = swap(send.astype(BF), 1)
    mine = keep + got.astype(F32)
    over = swap(mine[half:].astype(BF), 2)
    return mine[:half] + over.astype(F32)


def dp_swap(value, bit):
    count = lax.axis_size("dp")
    return lax.ppermute(value, "dp", [(i, i ^ (1 << bit)) for i in range(count)])


def dp_bits():
    count = lax.axis_size("dp")
    bits = count.bit_length() - 1
    assert 1 << bits == count
    return bits


def my_bit(bit):
    return (lax.axis_index("dp") >> bit) & 1


def reduce_scatter_dp(value, order):
    for bit in order:
        half = value.shape[0] // 2
        place = my_bit(bit)
        send = lax.dynamic_slice_in_dim(value, (1 - place) * half, half, 0)
        keep = lax.dynamic_slice_in_dim(value, place * half, half, 0)
        got = dp_swap(send, bit)
        value = (keep.astype(F32) + got.astype(F32)).astype(BF)
    return value


def join(mine, got, place):
    return jnp.where(
        place == 0,
        jnp.concatenate([mine, got], axis=0),
        jnp.concatenate([got, mine], axis=0),
    )


def all_gather_dp(value, order):
    for bit in reversed(order):
        value = join(value, dp_swap(value, bit), my_bit(bit))
    return value


def all_reduce_dp(value, order):
    return all_gather_dp(reduce_scatter_dp(value, order), order)


def normalize(values):
    mean = jnp.mean(values, axis=-1, keepdims=True)
    centred = values - mean
    spread = jnp.mean(centred * centred, axis=-1, keepdims=True)
    inverse = lax.rsqrt(spread + EPS)
    return centred * inverse, inverse


def norm_back(grad, unit, inverse, gain):
    g = grad * gain
    return inverse * (
        g
        - jnp.mean(g, axis=-1, keepdims=True)
        - unit * jnp.mean(g * unit, axis=-1, keepdims=True)
    )


def place_of(block, me):
    rel = block ^ me
    return ((rel & 1) << 1) | (rel >> 1)


def masked_distance(start_ref, block, rows):
    width = (block + 1) * rows
    query = block * rows + lax.broadcasted_iota(jnp.int32, (rows, width), 0)
    key = lax.broadcasted_iota(jnp.int32, (rows, width), 1)
    start = start_ref[block * rows : (block + 1) * rows, :]
    allowed = (key <= query) & (key >= start)
    return jnp.where(allowed, (query - key).astype(F32), FAR)


def forward_kernel(me_ref, slope_ref, start_ref, qkv_ref, ctx_ref, lse_ref, held):
    me = me_ref[0]
    total = qkv_ref.shape[0]
    rows = total // TENSOR
    heads = qkv_ref.shape[1] // (3 * HEAD)
    for block in range(TENSOR):
        spot = pl.multiple_of(place_of(block, me) * rows, rows)
        held[block * rows : (block + 1) * rows, :] = qkv_ref[pl.ds(spot, rows), :]
    for block in range(TENSOR):
        spot = pl.multiple_of(place_of(block, me) * rows, rows)
        width = (block + 1) * rows
        distance = masked_distance(start_ref, block, rows)
        for head in range(heads):
            at = head * 3 * HEAD
            query = held[block * rows : width, at : at + HEAD]
            key = held[:width, at + HEAD : at + 2 * HEAD]
            value = held[:width, at + 2 * HEAD : at + 3 * HEAD]
            scores = dot(query, key, 1, 1) * SCALE - slope_ref[head] * distance
            best = jnp.max(scores, axis=1, keepdims=True)
            weights = jnp.exp(scores - best)
            mass = jnp.sum(weights, axis=1, keepdims=True)
            out = dot(weights.astype(BF), value) / mass
            ctx_ref[pl.ds(spot, rows), head * HEAD : (head + 1) * HEAD] = out.astype(BF)
            lse_ref[block * rows : width, head : head + 1] = best + jnp.log(mass)


def backward_kernel(
    me_ref, slope_ref, start_ref, qkv_ref, outer_ref, lse_ref, grad_ref, held, outer, keys, values
):
    me = me_ref[0]
    total = qkv_ref.shape[0]
    rows = total // TENSOR
    heads = qkv_ref.shape[1] // (3 * HEAD)
    for block in range(TENSOR):
        spot = pl.multiple_of(place_of(block, me) * rows, rows)
        held[block * rows : (block + 1) * rows, :] = qkv_ref[pl.ds(spot, rows), :]
        outer[block * rows : (block + 1) * rows, :] = outer_ref[pl.ds(spot, rows), :]
    for block in reversed(range(TENSOR)):
        spot = pl.multiple_of(place_of(block, me) * rows, rows)
        width = (block + 1) * rows
        distance = masked_distance(start_ref, block, rows)
        for head in range(heads):
            at = head * 3 * HEAD
            cols = slice(head * HEAD, (head + 1) * HEAD)
            query = held[block * rows : width, at : at + HEAD]
            key = held[:width, at + HEAD : at + 2 * HEAD]
            value = held[:width, at + 2 * HEAD : at + 3 * HEAD]
            grad = outer[block * rows : width, cols]
            lse = lse_ref[block * rows : width, head : head + 1]
            scores = dot(query, key, 1, 1) * SCALE - slope_ref[head] * distance
            probs = jnp.exp(scores - lse)
            prob_grad = dot(grad, value, 1, 1)
            delta = jnp.sum(probs * prob_grad, axis=1, keepdims=True)
            score_grad = (probs * (prob_grad - delta)).astype(BF)
            key_part = dot(score_grad, query, 0, 0)
            value_part = dot(probs.astype(BF), grad, 0, 0)
            if block == TENSOR - 1:
                keys[:width, cols] = key_part
                values[:width, cols] = value_part
            else:
                keys[:width, cols] += key_part
                values[:width, cols] += value_part
            grad_ref[pl.ds(spot, rows), at : at + HEAD] = (dot(score_grad, key) * SCALE).astype(BF)
    for block in range(TENSOR):
        spot = pl.multiple_of(place_of(block, me) * rows, rows)
        part = slice(block * rows, (block + 1) * rows)
        for head in range(heads):
            at = head * 3 * HEAD
            cols = slice(head * HEAD, (head + 1) * HEAD)
            grad_ref[pl.ds(spot, rows), at + HEAD : at + 2 * HEAD] = (
                keys[part, cols] * SCALE
            ).astype(BF)
            grad_ref[pl.ds(spot, rows), at + 2 * HEAD : at + 3 * HEAD] = values[part, cols].astype(
                BF
            )


SMEM = pl.BlockSpec(memory_space=pltpu.SMEM)
VMEM = pl.BlockSpec(memory_space=pltpu.VMEM)


def attention(me, slopes, start, qkv):
    total, width = qkv.shape
    heads = width // (3 * HEAD)
    return pl.pallas_call(
        forward_kernel,
        name="attention_forward",
        out_shape=(
            jax.ShapeDtypeStruct((total, heads * HEAD), BF),
            jax.ShapeDtypeStruct((total, heads), F32),
        ),
        in_specs=[SMEM, SMEM, VMEM, VMEM],
        out_specs=(VMEM, VMEM),
        scratch_shapes=[pltpu.VMEM((total, width), BF)],
        compiler_params=pltpu.CompilerParams(vmem_limit_bytes=VMEM_LIMIT),
        cost_estimate=pl.CostEstimate(
            flops=4 * total * total * heads * HEAD,
            bytes_accessed=2 * total * width * 2,
            transcendentals=heads * total * total // 2,
        ),
    )(me, slopes, start, qkv)


def attention_back(me, slopes, start, qkv, outer, lse):
    total, width = qkv.shape
    heads = width // (3 * HEAD)
    return pl.pallas_call(
        backward_kernel,
        name="attention_backward",
        out_shape=jax.ShapeDtypeStruct((total, width), BF),
        in_specs=[SMEM, SMEM, VMEM, VMEM, VMEM, VMEM],
        out_specs=VMEM,
        scratch_shapes=[
            pltpu.VMEM((total, width), BF),
            pltpu.VMEM((total, heads * HEAD), BF),
            pltpu.VMEM((total, heads * HEAD), F32),
            pltpu.VMEM((total, heads * HEAD), F32),
        ],
        compiler_params=pltpu.CompilerParams(vmem_limit_bytes=VMEM_LIMIT),
        cost_estimate=pl.CostEstimate(
            flops=10 * total * total * heads * HEAD,
            bytes_accessed=4 * total * width * 2,
            transcendentals=heads * total * total // 2,
        ),
    )(me, slopes, start, qkv, outer, lse)


def per_device(
    tokens,
    cotangent,
    seq_lengths,
    ln1_gain,
    ln1_bias,
    qkv_weight,
    qv_bias,
    dense_weight,
    dense_bias,
    ln2_gain,
    ln2_bias,
    up_weight,
    up_bias,
    down_weight,
    down_bias,
):
    rows = tokens.shape[0]
    total = rows * TENSOR
    heads = qkv_weight.shape[1] // (3 * HEAD)
    wide = heads * HEAD
    bits = dp_bits()
    x_first = list(range(bits))
    z_first = x_first[1:] + x_first[:1]
    rank = lax.axis_index("tensor")
    me = rank.astype(jnp.int32).reshape(1)
    slopes = jnp.exp2(
        -8.0 * ((rank * heads + jnp.arange(heads, dtype=jnp.int32)).astype(F32) + 1.0) / H
    )
    ends = jnp.cumsum(seq_lengths[0])
    positions = jnp.arange(total, dtype=jnp.int32)
    start = jnp.max(
        jnp.where(ends[None, :] <= positions[:, None], ends[None, :], 0), axis=1, keepdims=True
    )
    gain1, shift1 = ln1_gain.astype(F32), ln1_bias.astype(F32)
    gain2, shift2 = ln2_gain.astype(F32), ln2_bias.astype(F32)

    inputs = tokens.astype(F32)
    unit1, inverse1 = normalize(inputs)
    norm1_parts = gather((unit1 * gain1 + shift1).astype(BF))
    norm1 = jnp.concatenate(norm1_parts, axis=0)
    pair = qv_bias.astype(F32).reshape(heads, 2, HEAD)
    bias_full = jnp.stack([pair[:, 0], jnp.zeros_like(pair[:, 0]), pair[:, 1]], axis=1).reshape(
        3 * wide
    )
    qkv = (dot(norm1, qkv_weight) + bias_full).astype(BF)

    cot_parts = gather(after(cotangent, norm1_parts[1]))
    spread = min(bits, 2)
    piece = dense_weight.shape[0] >> spread
    low_index = lax.axis_index("dp") & ((1 << spread) - 1)
    part = lax.dynamic_slice_in_dim(dense_weight, low_index * piece, piece, 0)
    across = swap(after(part, cot_parts[1]), 2)
    for bit in range(spread):
        across = join(across, dp_swap(across, bit), my_bit(bit))
    dense_full = jnp.concatenate(
        [dense_weight, across, swap(dense_weight, 1), swap(across, 1)], axis=0
    )
    cot = jnp.concatenate(cot_parts, axis=0)
    act_grad = dot(cot, down_weight, 1, 1)

    context, lse = attention(me, slopes, start, qkv)
    blocks = [context[i * rows : (i + 1) * rows] for i in range(TENSOR)]
    mixed_heads = jnp.concatenate(
        [blocks[0], swap(blocks[1], 2), swap(blocks[2], 1), swap(blocks[3], 3)], axis=1
    )
    resid = inputs + (dot(mixed_heads, dense_full) + dense_bias.astype(F32))

    unit2, inverse2 = normalize(resid)
    norm2 = jnp.concatenate(gather((unit2 * gain2 + shift2).astype(BF)), axis=0)
    hidden_pre = dot(norm2, up_weight) + up_bias.astype(F32)
    activated, gelu_pull = jax.vjp(lambda u: jax.nn.gelu(u, approximate=True), hidden_pre)
    activated = activated.astype(BF)
    pre_grad = gelu_pull(act_grad)[0].astype(BF)

    grad_down = dot(activated, cot, 0, 0).astype(BF)
    grad_up = dot(norm2, pre_grad, 0, 0).astype(BF)
    grad_down = all_reduce_dp(grad_down, x_first)
    grad_up = all_reduce_dp(grad_up, x_first)
    grad_up_bias = jnp.sum(pre_grad.astype(F32), axis=0)

    half = total // 2
    norm2_send = dot(pre_grad[half:], up_weight, 1, 1)
    norm2_keep = dot(pre_grad[:half], up_weight, 1, 1)
    norm2_grad = scatter_sum(norm2_keep, norm2_send)
    grad_gain2 = jnp.sum(norm2_grad * unit2, axis=0)
    grad_shift2 = jnp.sum(norm2_grad, axis=0)
    resid_grad = cotangent.astype(F32) + norm_back(norm2_grad, unit2, inverse2, gain2)
    resid_low = resid_grad.astype(BF)
    grad_dense_bias = jnp.sum(resid_low.astype(F32), axis=0)

    ctx_grad = dot(resid_low, dense_full, 1, 1).astype(BF)
    cols = [ctx_grad[:, i * wide : (i + 1) * wide] for i in range(TENSOR)]
    outer = jnp.concatenate(
        [cols[0], swap(cols[1], 2), swap(cols[2], 1), swap(cols[3], 3)], axis=0
    )
    qkv_grad = attention_back(me, slopes, start, qkv, outer, lse)

    resid_full = jnp.concatenate(gather(after(resid_low, outer)), axis=0)
    grad_dense = dot(context, resid_full, 0, 0).astype(BF)
    grad_dense = all_reduce_dp(grad_dense, x_first)

    mixed_send = dot(activated[half:], down_weight)
    mixed_keep = dot(activated[:half], down_weight)
    mixed = scatter_sum(mixed_keep, after(mixed_send, resid_full))
    output = (resid + mixed + down_bias.astype(F32)).astype(BF)

    grad_qkv = dot(norm1, qkv_grad, 0, 0).astype(BF)
    grad_qkv = all_reduce_dp(grad_qkv, x_first)
    slot_sums = jnp.sum(qkv_grad.astype(F32), axis=0).reshape(heads, 3, HEAD)
    grad_qv_bias = jnp.stack([slot_sums[:, 0], slot_sums[:, 2]], axis=1).reshape(2 * wide)
    norm1_send = dot(qkv_grad[half:], qkv_weight, 1, 1)
    norm1_keep = dot(qkv_grad[:half], qkv_weight, 1, 1)
    norm1_grad = scatter_sum(norm1_keep, norm1_send)
    grad_gain1 = jnp.sum(norm1_grad * unit1, axis=0)
    grad_shift1 = jnp.sum(norm1_grad, axis=0)
    grad_tokens = (resid_grad + norm_back(norm1_grad, unit1, inverse1, gain1)).astype(BF)

    grad_down_bias = jnp.sum(cotangent.astype(F32), axis=0)
    shared = jnp.stack(
        [grad_gain1, grad_shift1, grad_dense_bias, grad_gain2, grad_shift2, grad_down_bias]
    )
    shared = shared + swap(shared, 1)
    shared = shared + swap(shared, 2)
    width = shared.shape[1]
    flat = jnp.concatenate([grad_up_bias, grad_qv_bias])
    own = jnp.pad(flat, (0, -flat.shape[0] % width)).reshape(-1, width)
    small = jnp.concatenate([shared, own], axis=0)
    for bit in range(bits):
        small = small + dp_swap(small, bit)
    flat_sum = small[6:].reshape(-1)
    return (
        output,
        grad_tokens,
        small[0],
        small[1],
        grad_qkv.astype(F32),
        flat_sum[grad_up_bias.shape[0] : flat.shape[0]],
        grad_dense.astype(F32),
        small[2],
        small[3],
        small[4],
        grad_up.astype(F32),
        flat_sum[: grad_up_bias.shape[0]],
        grad_down.astype(F32),
        small[5],
    )


def solution(mesh):
    return jax.shard_map(
        per_device,
        mesh=mesh,
        in_specs=(
            P(("dp", "tensor"), None),
            P(("dp", "tensor"), None),
            P("dp", None),
            P(),
            P(),
            P(None, "tensor"),
            P("tensor"),
            P("tensor", None),
            P(),
            P(),
            P(),
            P(None, "tensor"),
            P("tensor"),
            P("tensor", None),
            P(),
        ),
        out_specs=(
            P(("dp", "tensor"), None),
            P(("dp", "tensor"), None),
            P(),
            P(),
            P(None, "tensor"),
            P("tensor"),
            P("tensor", None),
            P(),
            P(),
            P(),
            P(None, "tensor"),
            P("tensor"),
            P("tensor", None),
            P(),
        ),
        check_vma=False,
    )
```

```python
import functools
import math

import jax
import jax.numpy as jnp
from jax import lax
from jax.experimental import pallas as pl
from jax.experimental.pallas import tpu as pltpu
from jax.sharding import PartitionSpec as P

H = 16
HEAD = 64
EPS = 1e-05
FAR = 1e34
BF = jnp.bfloat16
F32 = jnp.float32
SCALE = 1.0 / math.sqrt(HEAD)
TENSOR = 4


def dot(left, right, left_dim=1, right_dim=0):
    return lax.dot_general(
        left, right, (((left_dim,), (right_dim,)), ((), ())), preferred_element_type=F32
    )


def after(values, *earlier):
    return lax.optimization_barrier((values,) + earlier)[0]


def swap(value, mask):
    return lax.ppermute(value, "tensor", [(i, i ^ mask) for i in range(TENSOR)])


def dp_swap(value, bit):
    count = lax.axis_size("dp")
    return lax.ppermute(value, "dp", [(i, i ^ (1 << bit)) for i in range(count)])


def dp_bits():
    count = lax.axis_size("dp")
    bits = count.bit_length() - 1
    assert 1 << bits == count
    return bits


def my_bit(bit):
    return (lax.axis_index("dp") >> bit) & 1


def join(mine, got, place):
    return jnp.where(
        place == 0,
        jnp.concatenate([mine, got], axis=0),
        jnp.concatenate([got, mine], axis=0),
    )


def split_kernel(place_ref, keep_ref, got_ref, *out_refs):
    rows = keep_ref.shape[0]
    if len(out_refs) == 1:
        out_refs[0][...] = (keep_ref[...].astype(F32) + got_ref[...].astype(F32)).astype(BF)
        return
    half = rows // 2
    for out, place in zip(out_refs, (1 - place_ref[0], place_ref[0])):
        spot = pl.ds(pl.multiple_of(place * half, half), half)
        out[...] = (keep_ref[spot, :].astype(F32) + got_ref[spot, :].astype(F32)).astype(BF)


def place_kernel(index_ref, *refs):
    rows = refs[0].shape[0]
    for k, ref in enumerate(refs[:-1]):
        spot = index_ref[0] ^ k
        refs[-1][pl.ds(pl.multiple_of(spot * rows, rows), rows), :] = ref[...]


def join_kernel(place_ref, mine_ref, got_ref, out_ref):
    rows = mine_ref.shape[0]
    place = place_ref[0]
    mine = pl.ds(pl.multiple_of(place * rows, rows), rows)
    got = pl.ds(pl.multiple_of((1 - place) * rows, rows), rows)
    out_ref[mine, :] = mine_ref[...].astype(out_ref.dtype)
    out_ref[got, :] = got_ref[...].astype(out_ref.dtype)


class DpSum:
    def __init__(self, name, send, keep, order):
        self.name = name
        self.plan = [("sum", bit) for bit in order] + [("join", bit) for bit in reversed(order)]
        self.exchange(send, keep)

    def exchange(self, send, keep):
        kind, bit = self.plan[0]
        self.keep = keep
        with jax.named_scope(f"{self.name}_{kind}_{bit}"):
            self.got = dp_swap(send, bit)

    def step(self, *earlier):
        kind, bit = self.plan.pop(0)
        got = after(self.got, *earlier)
        rows, cols = self.keep.shape
        if kind == "join":
            last = not self.plan
            place = my_bit(bit).astype(jnp.int32).reshape(1)
            if rows % 16:
                value = join(self.keep, got, my_bit(bit))
            else:
                (value,) = run(
                    self.name + "_join", join_kernel, [((2 * rows, cols), F32 if last else BF)],
                    [place], [self.keep, got],
                )
            self.value = value
            if not last:
                self.exchange(value, value)
            return value
        following, next_bit = self.plan[0]
        place = my_bit(next_bit).astype(jnp.int32).reshape(1)
        if rows % 32:
            value = (self.keep.astype(F32) + got.astype(F32)).astype(BF)
            out = [value]
            if following == "sum":
                out = [
                    lax.dynamic_slice_in_dim(value, spot * (rows // 2), rows // 2, 0)
                    for spot in (1 - my_bit(next_bit), my_bit(next_bit))
                ]
            self.exchange(out[0], out[-1])
            return out[-1]
        shapes = [((rows // 2, cols), BF)] * 2 if following == "sum" else [((rows, cols), BF)]
        out = run(self.name + "_add", split_kernel, shapes, [place], [self.keep, got])
        self.exchange(out[0], out[-1])
        return out[-1]


SMEM = pl.BlockSpec(memory_space=pltpu.SMEM)
VMEM = pl.BlockSpec(memory_space=pltpu.VMEM)


def params(mib):
    return pltpu.CompilerParams(vmem_limit_bytes=mib * 1024 * 1024)


def run(name, body, outs, scalars, arrays, mib=6, far=(), scratch=()):
    n_first = len(scalars)
    n_in = n_first + len(arrays)
    n_refs = n_in + len(outs) + len(scratch)

    def fetching(*refs):
        refs, held, sems = list(refs[:n_refs]), refs[n_refs:-1], refs[-1]
        copies = [
            pltpu.make_async_copy(refs[n_first + at], spot, sems.at[i])
            for i, (at, spot) in enumerate(zip(far, held))
        ]
        for copy in copies:
            copy.start()
        for copy in copies:
            copy.wait()
        for at, spot in zip(far, held):
            refs[n_first + at] = spot
        body(*refs)

    specs = [VMEM] * len(arrays)
    scratch = list(scratch)
    for at in far:
        specs[at] = pl.BlockSpec(memory_space=pl.ANY)
        scratch.append(pltpu.VMEM(arrays[at].shape, arrays[at].dtype))
    if far:
        scratch.append(pltpu.SemaphoreType.DMA((len(far),)))
    return pl.pallas_call(
        fetching if far else body,
        name=name,
        out_shape=[jax.ShapeDtypeStruct(shape, dtype) for shape, dtype in outs],
        in_specs=[SMEM] * len(scalars) + specs,
        out_specs=[VMEM] * len(outs),
        scratch_shapes=scratch,
        compiler_params=params(mib),
        cost_estimate=pl.CostEstimate(flops=1, bytes_accessed=1, transcendentals=0),
    )(*scalars, *arrays)


def normalize(values):
    mean = jnp.mean(values, axis=-1, keepdims=True)
    centred = values - mean
    spread = jnp.mean(centred * centred, axis=-1, keepdims=True)
    inverse = lax.rsqrt(spread + EPS)
    return centred * inverse, inverse


def norm_back(grad, unit, inverse, gain):
    g = grad * gain
    return inverse * (
        g
        - jnp.mean(g, axis=-1, keepdims=True)
        - unit * jnp.mean(g * unit, axis=-1, keepdims=True)
    )


def masked_distance(start_ref, block, rows):
    width = (block + 1) * rows
    query = block * rows + lax.broadcasted_iota(jnp.int32, (rows, width), 0)
    key = lax.broadcasted_iota(jnp.int32, (rows, width), 1)
    start = start_ref[block * rows : (block + 1) * rows, :]
    allowed = (key <= query) & (key >= start)
    return jnp.where(allowed, (query - key).astype(F32), FAR)


def spot_of(k, me, rows):
    return pl.ds(pl.multiple_of((k ^ me) * rows, rows), rows)


def forward_kernel(
    me_ref, slope_ref, start_ref, weight_ref, bias_ref, gain_ref, shift_ref, *refs,
):
    token_refs, refs = refs[:TENSOR], refs[TENSOR:]
    ctx_refs, (full_ref, lse_ref, held, norm_ref, made) = refs[:TENSOR], refs[TENSOR:]
    me = me_ref[0]
    rows = token_refs[0].shape[0]
    heads = weight_ref.shape[1] // (3 * HEAD)
    for k, ref in enumerate(token_refs):
        unit, _ = normalize(ref[...].astype(F32))
        norm = (unit * gain_ref[...] + shift_ref[...]).astype(BF)
        norm_ref[k * rows : (k + 1) * rows, :] = norm
        made_qkv = dot(norm, weight_ref[...]) + bias_ref[...]
        held[spot_of(k, me, rows), :] = made_qkv.astype(BF)
    for block in range(TENSOR):
        width = (block + 1) * rows
        distance = masked_distance(start_ref, block, rows)
        for head in range(heads):
            at = head * 3 * HEAD
            query = held[block * rows : width, at : at + HEAD]
            key = held[:width, at + HEAD : at + 2 * HEAD]
            value = held[:width, at + 2 * HEAD : at + 3 * HEAD]
            scores = dot(query, key, 1, 1) * SCALE - slope_ref[head] * distance
            best = jnp.max(scores, axis=1, keepdims=True)
            weights = jnp.exp(scores - best)
            mass = jnp.sum(weights, axis=1, keepdims=True)
            out = dot(weights.astype(BF), value) / mass
            made[block * rows : width, head * HEAD : (head + 1) * HEAD] = out.astype(BF)
            lse_ref[block * rows : width, head : head + 1] = best + jnp.log(mass)
    for k in range(TENSOR):
        part = made[spot_of(k, me, rows), :]
        ctx_refs[k][...] = part
        full_ref[k * rows : (k + 1) * rows, :] = part


def backward_kernel(me_ref, slope_ref, start_ref, lse_ref, held, *refs):
    outer_refs, (grad_ref, outer, keys, values, made) = refs[:TENSOR], refs[TENSOR:]
    me = me_ref[0]
    rows = held.shape[0] // TENSOR
    heads = held.shape[1] // (3 * HEAD)
    for k in range(TENSOR):
        outer[spot_of(k, me, rows), :] = outer_refs[k][...]
    for block in reversed(range(TENSOR)):
        width = (block + 1) * rows
        distance = masked_distance(start_ref, block, rows)
        for head in range(heads):
            at = head * 3 * HEAD
            cols = slice(head * HEAD, (head + 1) * HEAD)
            query = held[block * rows : width, at : at + HEAD]
            key = held[:width, at + HEAD : at + 2 * HEAD]
            value = held[:width, at + 2 * HEAD : at + 3 * HEAD]
            grad = outer[block * rows : width, cols]
            lse = lse_ref[block * rows : width, head : head + 1]
            scores = dot(query, key, 1, 1) * SCALE - slope_ref[head] * distance
            probs = jnp.exp(scores - lse)
            prob_grad = dot(grad, value, 1, 1)
            delta = jnp.sum(probs * prob_grad, axis=1, keepdims=True)
            score_grad = (probs * (prob_grad - delta)).astype(BF)
            key_part = dot(score_grad, query, 0, 0)
            value_part = dot(probs.astype(BF), grad, 0, 0)
            if block == TENSOR - 1:
                keys[:width, cols] = key_part
                values[:width, cols] = value_part
            else:
                keys[:width, cols] += key_part
                values[:width, cols] += value_part
            made[block * rows : width, at : at + HEAD] = (dot(score_grad, key) * SCALE).astype(BF)
    for head in range(heads):
        at = head * 3 * HEAD
        cols = slice(head * HEAD, (head + 1) * HEAD)
        made[:, at + HEAD : at + 2 * HEAD] = (keys[:, cols] * SCALE).astype(BF)
        made[:, at + 2 * HEAD : at + 3 * HEAD] = values[:, cols].astype(BF)
    for k in range(TENSOR):
        grad_ref[k * rows : (k + 1) * rows, :] = made[spot_of(k, me, rows), :]


def attention(me, slopes, start, weight, bias, gain, shift, tokens):
    rows, model = tokens[0].shape
    width = weight.shape[1]
    total = rows * TENSOR
    wide = width // 3
    out = run(
        "attention_forward",
        forward_kernel,
        [((rows, wide), BF)] * TENSOR
        + [
            ((total, wide), BF),
            ((total, wide // HEAD), F32),
            ((total, width), BF),
            ((total, model), BF),
        ],
        [me, slopes],
        [start, weight, bias[None], gain[None], shift[None], *tokens],
        22,
        far=(1, 5, 6, 7, 8),
        scratch=[pltpu.VMEM((total, wide), BF)],
    )
    return out[:TENSOR], *out[TENSOR:]


def attention_back(me, slopes, start, lse, held, outer):
    total, width = held.shape
    wide = width // 3
    return run(
        "attention_backward",
        backward_kernel,
        [((total, width), BF)],
        [me, slopes],
        [start, lse, held, *outer],
        26,
        far=(2, 3, 4, 5, 6),
        scratch=[
            pltpu.VMEM((total, wide), BF),
            pltpu.VMEM((total, wide), F32),
            pltpu.VMEM((total, wide), F32),
            pltpu.VMEM((total, width), BF),
        ],
    )[0]


def norm2_back_kernel(
    part_ref, beside_ref, across_ref, unit_ref, inverse_ref, gain_ref, cot_ref, *refs
):
    weight_refs, (resid_ref, low_ref, sums_ref), ctx_refs = (
        refs[:TENSOR],
        refs[TENSOR : TENSOR + 3],
        refs[TENSOR + 3 :],
    )
    rows = beside_ref.shape[0]
    grad = (
        part_ref[:rows, :].astype(F32)
        + beside_ref[...].astype(F32)
        + across_ref[...].astype(F32)
    )
    unit = unit_ref[...]
    resid = cot_ref[...].astype(F32) + norm_back(grad, unit, inverse_ref[...], gain_ref[...])
    low = resid.astype(BF)
    resid_ref[...] = resid
    low_ref[...] = low
    sums_ref[0:1, :] = jnp.sum(grad * unit, axis=0, keepdims=True)
    sums_ref[1:2, :] = jnp.sum(grad, axis=0, keepdims=True)
    sums_ref[2:3, :] = jnp.sum(low.astype(F32), axis=0, keepdims=True)
    sums_ref[3:4, :] = jnp.sum(cot_ref[...].astype(F32), axis=0, keepdims=True)
    for ctx, weight in zip(ctx_refs, weight_refs):
        ctx[...] = dot(low, weight[...], 1, 1).astype(BF)


def norm2_back(part, beside, across, unit, inverse, gain, cot, weights):
    rows, width = beside.shape
    out = run(
        "norm2_back",
        norm2_back_kernel,
        [((rows, width), F32), ((rows, width), BF), ((4, width), F32)]
        + [((rows, weight.shape[0]), BF) for weight in weights],
        [],
        [part, beside, across, unit, inverse, gain[None], cot, *weights],
        10,
        far=(1, 2, 6, 7, 8, 9, 10),
    )
    return out[0], out[1], out[2], out[3:]


def norm1_part_kernel(qkv_ref, weight_ref, *refs):
    token_refs, part_refs, sums_ref = refs[:TENSOR], refs[TENSOR:-1], refs[-1]
    rows = token_refs[0].shape[0]
    gain_sum, shift_sum = 0.0, 0.0
    for k, (tokens, part) in enumerate(zip(token_refs, part_refs)):
        grad = dot(qkv_ref[k * rows : (k + 1) * rows, :], weight_ref[...], 1, 1)
        part[...] = grad.astype(BF)
        unit, _ = normalize(tokens[...].astype(F32))
        gain_sum += jnp.sum(grad * unit, axis=0, keepdims=True)
        shift_sum += jnp.sum(grad, axis=0, keepdims=True)
    sums_ref[0:1, :] = gain_sum
    sums_ref[1:2, :] = shift_sum


def norm1_part(qkv_grad, weight, tokens):
    shape = tokens[0].shape
    out = run(
        "norm1_part",
        norm1_part_kernel,
        [(shape, BF)] * TENSOR + [((2, shape[1]), F32)],
        [],
        [qkv_grad, weight, *tokens],
        10,
        far=(1, 2, 3, 4, 5),
    )
    return out[:TENSOR], out[TENSOR]


def norm1_back_kernel(*refs):
    part_refs, (tokens_ref, gain_ref, resid_ref, grad_ref) = refs[:TENSOR], refs[TENSOR:]
    grad = part_refs[0][...].astype(F32)
    for ref in part_refs[1:]:
        grad += ref[...].astype(F32)
    unit, inverse = normalize(tokens_ref[...].astype(F32))
    grad_ref[...] = (
        resid_ref[...] + norm_back(grad, unit, inverse, gain_ref[...])
    ).astype(BF)


def norm1_back(parts, tokens, gain, resid):
    return run(
        "norm1_back",
        norm1_back_kernel,
        [(tokens.shape, BF)],
        [],
        [*parts, tokens, gain[None], resid],
        12,
        far=(0, 1, 2, 3, 4, 6),
    )[0]


def dense_kernel(tokens_ref, bias_ref, gain_ref, shift_ref, *refs):
    heads_refs, refs = refs[:TENSOR], refs[TENSOR:]
    weight_refs, (resid_ref, norm_ref, unit_ref, inverse_ref) = refs[:TENSOR], refs[TENSOR:]
    total = dot(heads_refs[0][...], weight_refs[0][...])
    for k in range(1, TENSOR):
        total += dot(heads_refs[k][...], weight_refs[k][...])
    resid = tokens_ref[...].astype(F32) + (total + bias_ref[...])
    unit, inverse = normalize(resid)
    resid_ref[...] = resid
    unit_ref[...] = unit
    inverse_ref[...] = inverse
    norm_ref[...] = (unit * gain_ref[...] + shift_ref[...]).astype(BF)


def dense_norm(tokens, bias, gain, shift, mixed, weights):
    rows, width = tokens.shape
    return run(
        "dense_norm",
        dense_kernel,
        [((rows, width), F32), ((rows, width), BF), ((rows, width), F32), ((rows, 1), F32)],
        [],
        [tokens, bias[None], gain[None], shift[None], *mixed, *weights],
        10,
        far=(0, 4, 5, 6, 7, 8, 9, 10, 11),
    )


ROOT = math.sqrt(2.0 / math.pi)
CUBE = 0.044715


def feed_kernel(first_ref, second_ref, weight_ref, bias_ref, grad_ref, act_ref, pre_ref):
    rows = first_ref.shape[0]
    wide = min(256, weight_ref.shape[1])
    for i, ref in enumerate((first_ref, second_ref)):
        part = slice(i * rows, (i + 1) * rows)
        for at in range(0, weight_ref.shape[1], wide):
            cols = slice(at, at + wide)
            u = dot(ref[...], weight_ref[:, cols]) + bias_ref[:, cols]
            square = u * u
            bent = jnp.tanh(ROOT * (u + CUBE * (square * u)))
            half = 0.5 * (1.0 + bent)
            act_ref[part, cols] = (u * half).astype(BF)
            slope = half + 0.5 * u * (1.0 - bent * bent) * (ROOT + (3.0 * CUBE * ROOT) * square)
            pre_ref[part, cols] = (grad_ref[part, cols] * slope).astype(BF)


def feed(first, second, weight, bias, act_grad):
    shape = (2 * first.shape[0], weight.shape[1])
    return run(
        "feed_forward",
        feed_kernel,
        [(shape, BF)] * 2,
        [],
        [first, second, weight, bias[None], act_grad],
        12,
        far=(0, 1, 2),
    )


def rows_kernel(first_ref, second_ref, weight_ref, out_ref):
    rows = first_ref.shape[0]
    out_ref[:rows, :] = dot(first_ref[...], weight_ref[...], 1, 1)
    out_ref[rows:, :] = dot(second_ref[...], weight_ref[...], 1, 1)


def act_gradient(first, second, weight):
    shape = (2 * first.shape[0], weight.shape[0])
    return run("act_grad", rows_kernel, [(shape, F32)], [], [first, second, weight], 8)[0]


def part_kernel(side, value_ref, weight_ref, keep_ref, send_ref):
    rows = keep_ref.shape[0]
    keep_ref[...] = dot(value_ref[:rows, :], weight_ref[...], 1, side).astype(BF)
    send_ref[...] = dot(value_ref[rows:, :], weight_ref[...], 1, side).astype(BF)


def partial_rows(name, value, weight, side):
    shape = (value.shape[0] // 2, weight.shape[1 - side])
    body = functools.partial(part_kernel, side)
    return run(name, body, [(shape, BF)] * 2, [], [value, weight], 8)


def row_chunks(refs, rows):
    out = []
    for ref in refs:
        for at in range(0, ref.shape[0], rows):
            out.append((ref, slice(at, at + rows)))
    return out


def gradient_kernel(pieces, n_left, n_right, n_base, sums, places_ref, *refs):
    left, refs = refs[:n_left], refs[n_left:]
    right, refs = refs[:n_right], refs[n_right:]
    base, refs = refs[:n_base], refs[n_base:]
    rows = min(ref.shape[0] for ref in left + right)
    left = row_chunks(left, rows)
    right = row_chunks(right, rows)
    if pieces is None:
        height = refs[0].shape[0]
        pieces = [(0, height, None)]
    out = 0
    for first, height, bit in pieces:
        half = height if bit is None else height // 2
        step = min(256, half)
        for place in (None,) if bit is None else (1 - places_ref[bit], places_ref[bit]):
            for at in range(0, half, step):
                if place is None:
                    spot = pl.ds(first + at, step)
                else:
                    spot = pl.ds(pl.multiple_of(first + place * half + at, step), step)
                total = base[0][spot, :] if base else None
                for (l_ref, l_rows), (r_ref, r_rows) in zip(left, right):
                    term = dot(l_ref[l_rows, spot], r_ref[r_rows, :], 0, 0)
                    total = term if total is None else total + term
                refs[out][at : at + step, :] = total.astype(refs[out].dtype)
            out += 1
    if sums:
        total = None
        for ref, part in right:
            term = jnp.sum(ref[part, :].astype(F32), axis=0, keepdims=True)
            total = term if total is None else total + term
        refs[out][...] = total


def gradient(name, places, left, right, pieces, base=(), sums=False, mib=12):
    height, cols = left[0].shape[1], right[0].shape[1]
    if pieces is None:
        outs = [((height, cols), F32)]
    else:
        outs = [((rows // 2, cols), BF) for _, rows, _ in pieces for _ in range(2)]
    if sums:
        outs.append(((1, cols), F32))
    body = functools.partial(
        gradient_kernel, pieces, len(left), len(right), len(base), sums
    )
    return run(name, body, outs, [places], [*left, *right, *base], mib)


def output_kernel(resid_ref, bias_ref, *refs):
    mixed = refs[0][...].astype(F32)
    for ref in refs[1:-1]:
        mixed += ref[...].astype(F32)
    refs[-1][...] = (resid_ref[...] + (mixed + bias_ref[...])).astype(BF)


def pack_kernel(context_ref, *refs):
    resid_refs, (small_ref, out_ref) = refs[:TENSOR], refs[TENSOR:]
    rows = resid_refs[0].shape[0]
    height = context_ref.shape[1]
    total = dot(context_ref[:rows, :], resid_refs[0][...], 0, 0)
    for k in range(1, TENSOR):
        total += dot(context_ref[k * rows : (k + 1) * rows, :], resid_refs[k][...], 0, 0)
    out_ref[:height, :] = total.astype(BF)
    tail = out_ref.shape[0] - height - small_ref.shape[0]
    out_ref[height:, :] = jnp.concatenate(
        [small_ref[...], jnp.zeros((tail, small_ref.shape[1]), F32)], axis=0
    ).astype(BF)


def add_kernel(first_ref, second_ref, out_ref):
    out_ref[...] = (first_ref[...].astype(F32) + second_ref[...].astype(F32)).astype(BF)


def add_rows(first, second):
    return run("add_rows", add_kernel, [(first.shape, BF)], [], [first, second])[0]


def per_device(
    tokens,
    cotangent,
    seq_lengths,
    ln1_gain,
    ln1_bias,
    qkv_weight,
    qv_bias,
    dense_weight,
    dense_bias,
    ln2_gain,
    ln2_bias,
    up_weight,
    up_bias,
    down_weight,
    down_bias,
):
    rows = tokens.shape[0]
    total = rows * TENSOR
    heads = qkv_weight.shape[1] // (3 * HEAD)
    wide = heads * HEAD
    bits = dp_bits()
    x_first = list(range(bits))
    mixed_order = x_first[1::-1] + x_first[2:]
    rank = lax.axis_index("tensor")
    me = rank.astype(jnp.int32).reshape(1)
    slopes = jnp.exp2(
        -8.0 * ((rank * heads + jnp.arange(heads, dtype=jnp.int32)).astype(F32) + 1.0) / H
    )
    ends = jnp.cumsum(seq_lengths[0])
    positions = jnp.arange(total, dtype=jnp.int32)
    start = jnp.max(
        jnp.where(ends[None, :] <= positions[:, None], ends[None, :], 0), axis=1, keepdims=True
    )
    gain1, shift1 = ln1_gain.astype(F32), ln1_bias.astype(F32)
    gain2, shift2 = ln2_gain.astype(F32), ln2_bias.astype(F32)

    places = jnp.stack([my_bit(bit) for bit in range(bits)]).astype(jnp.int32)
    shares = 1 << min(bits, 2)
    piece = dense_weight.shape[0] // shares
    low_index = (lax.axis_index("dp") & (shares - 1)).astype(jnp.int32)
    part = swap(lax.dynamic_slice_in_dim(dense_weight, low_index * piece, piece, 0), 2)
    tokens_2 = swap(tokens, 2)
    tokens_1 = swap(tokens, 1)
    pair = qv_bias.astype(F32).reshape(heads, 2, HEAD)
    bias_full = jnp.stack([pair[:, 0], jnp.zeros_like(pair[:, 0]), pair[:, 1]], axis=1).reshape(
        3 * wide
    )
    cot_1 = swap(cotangent, 1)
    dense_1 = swap(dense_weight, 1)
    tokens_2, tokens_1, cot_1, dense_1, part, start, bias_full, slopes = lax.optimization_barrier(
        (tokens_2, tokens_1, cot_1, dense_1, part, start, bias_full, slopes)
    )
    tokens_3 = swap(tokens_2, 1)
    cot_2 = swap(after(cotangent, tokens_2), 2)
    count = lax.axis_size("dp")
    shared_parts = [part] + [
        lax.ppermute(part, "dp", [(i, i ^ k) for i in range(count)]) for k in range(1, shares)
    ]
    all_tokens = (tokens, tokens_1, tokens_2, tokens_3)
    blocks, context, lse, held, norm1 = attention(
        me, slopes, start, qkv_weight, bias_full, gain1, shift1, all_tokens
    )
    mixed_3 = swap(blocks[3], 3)
    mixed_2 = swap(blocks[2], 2)
    mixed_1 = swap(blocks[1], 1)
    *shared_parts, cot_2, _ = lax.optimization_barrier((*shared_parts, cot_2, context))
    (dense_2,) = run(
        "dense_rows",
        place_kernel,
        [(dense_weight.shape, BF)],
        [low_index.reshape(1)],
        list(shared_parts),
    )
    dense_3 = swap(dense_2, 1)
    dense = [dense_weight, dense_1, dense_2, dense_3]
    cot_3 = swap(cot_2, 1)
    act_grad_a = act_gradient(after(cotangent, dense_2), cot_1, down_weight)
    mixed = lax.optimization_barrier((blocks[0], mixed_1, mixed_2, mixed_3, act_grad_a))[:TENSOR]
    resid, norm2_0, unit2, inverse2 = dense_norm(
        tokens, dense_bias.astype(F32), gain2, shift2, mixed, dense
    )

    norm2_2 = swap(norm2_0, 2)
    norm2_1 = swap(norm2_0, 1)
    up_shift = up_bias.astype(F32)
    act_a, pre_a = feed(norm2_0, norm2_1, up_weight, up_shift, act_grad_a)
    act_grad_b = act_gradient(after(cot_2, act_a), cot_3, down_weight)
    (down_a,) = gradient("down_a", places, [act_a], [cotangent, cot_1], None)
    norm2_2 = lax.optimization_barrier((norm2_2, act_grad_b, down_a))[0]
    norm2_3 = swap(norm2_2, 1)
    act_b, pre_b = feed(norm2_2, norm2_3, up_weight, up_shift, act_grad_b)

    units = down_weight.shape[0]
    down_send, down_keep = gradient(
        "down", places, [act_b], [cot_2, cot_3], [(0, units, x_first[0])], [down_a]
    )
    down_sum = DpSum("down", down_send, down_keep, x_first)
    keep_b, send_b = partial_rows("norm2_part_b", after(pre_b, down_keep), up_weight, 1)
    beside_b = swap(send_b, 1)
    model = up_weight.shape[0]
    norms = [norm2_0, norm2_1, norm2_2, norm2_3]
    up_send, up_keep, up_shift_grad = gradient(
        "up", places, norms, [pre_a, after(pre_b, keep_b)], [(0, model, mixed_order[0])], sums=True
    )
    across = swap(add_rows(keep_b, after(beside_b, up_keep)), 2)
    up_sum = DpSum("up", up_send, up_keep, mixed_order)
    keep_a, send_a = partial_rows("norm2_part_a", after(pre_a, up_keep), up_weight, 1)
    beside_a = swap(send_a, 1)
    out_keep_b, out_send_b = partial_rows("out_part_b", after(act_b, keep_a), down_weight, 0)
    out_keep_a, out_send_a = partial_rows("out_part_a", after(act_a, keep_a), down_weight, 0)
    across = lax.optimization_barrier((across, out_keep_a, out_keep_b))[0]
    resid_grad, resid_low, sums2, ctx_grad = norm2_back(
        keep_a, beside_a, across, unit2, inverse2, gain2, cotangent, dense
    )

    outer_3 = swap(ctx_grad[3], 3)
    outer_2 = swap(ctx_grad[2], 2)
    outer_1 = swap(ctx_grad[1], 1)
    resid_1 = swap(resid_low, 1)
    outer = lax.optimization_barrier((ctx_grad[0], outer_1, outer_2, outer_3))
    last = down_sum.step(*outer)
    last = up_sum.step(last)
    outer = lax.optimization_barrier((*outer, last))[:TENSOR]
    resid_2 = swap(after(resid_low, *outer), 2)
    qkv_grad = attention_back(me, slopes, start, lse, held, outer)

    last = down_sum.step(qkv_grad)
    last = up_sum.step(last)
    qkv_send, qkv_keep, slot_sums = gradient(
        "qkv", places, [norm1], [after(qkv_grad, last)], [(0, model, x_first[0])], sums=True
    )
    qkv_sum = DpSum("qkv", qkv_send, qkv_keep, x_first)
    resid_2 = after(resid_2, qkv_keep)
    resid_3 = swap(resid_2, 1)
    parts, sums1 = norm1_part(after(qkv_grad, qkv_keep), qkv_weight, all_tokens)
    sums1 = after(sums1, down_sum.step(sums1))

    slot_sums = slot_sums.reshape(heads, 3, HEAD)
    grad_qv_bias = jnp.stack([slot_sums[:, 0], slot_sums[:, 2]], axis=1).reshape(2 * wide)
    shared = jnp.concatenate([sums1, sums2], axis=0)
    shared = shared + swap(shared, 1)
    shared = shared + swap(shared, 2)
    flat = jnp.concatenate([up_shift_grad.reshape(-1), grad_qv_bias])
    own = jnp.pad(flat, (0, -flat.shape[0] % model)).reshape(-1, model)
    small = jnp.concatenate([shared, own], axis=0)
    (packed,) = run(
        "dense",
        pack_kernel,
        [((wide + 128, model), BF)],
        [],
        [context, resid_low, resid_1, resid_2, resid_3, small],
        far=(0, 1, 2, 3, 4),
    )
    place = my_bit(mixed_order[0])
    half = packed.shape[0] // 2
    dense_sum = DpSum(
        "dense",
        lax.dynamic_slice_in_dim(packed, (1 - place) * half, half, 0),
        lax.dynamic_slice_in_dim(packed, place * half, half, 0),
        mixed_order,
    )
    parts = lax.optimization_barrier((*parts, dense_sum.keep))[:TENSOR]
    part_3 = swap(parts[3], 3)
    part_2 = swap(parts[2], 2)
    part_1 = swap(parts[1], 1)
    out_3 = swap(after(out_send_b, part_2), 3)
    out_2 = swap(after(out_keep_b, part_2), 2)
    out_1 = swap(after(out_send_a, part_1), 1)

    last = up_sum.step(dense_sum.keep)
    last = qkv_sum.step(last)
    last = down_sum.step(last)
    last = qkv_sum.step(last)
    last = dense_sum.step(last)
    last = up_sum.step(last)
    parts = lax.optimization_barrier((parts[0], part_1, part_2, part_3, last))[:TENSOR]
    grad_tokens = norm1_back(parts, tokens, gain1, resid_grad)
    last = dense_sum.step(grad_tokens)
    last = qkv_sum.step(last)
    last = down_sum.step(last)
    last = dense_sum.step(last)
    last = qkv_sum.step(last)
    last = dense_sum.step(last)
    mixed = lax.optimization_barrier((out_keep_a, out_1, out_2, out_3, last))[:TENSOR]
    (output,) = run(
        "output",
        output_kernel,
        [(resid.shape, BF)],
        [],
        [resid, down_bias.astype(F32)[None], *mixed],
        12,
        far=(0, 2, 3, 4, 5),
    )
    last = output
    order = [up_sum, dense_sum, qkv_sum, down_sum, dense_sum, up_sum, qkv_sum]
    while any(item.plan for item in order):
        for item in order:
            if item.plan:
                last = item.step(last)
        order = [dense_sum, qkv_sum, up_sum, down_sum]
    small = dense_sum.value[wide:]
    flat_sum = small[6 : 6 + own.shape[0]].reshape(-1)
    count = up_shift_grad.shape[1]
    return (
        output,
        grad_tokens,
        small[0],
        small[1],
        qkv_sum.value,
        flat_sum[count : flat.shape[0]],
        dense_sum.value[:wide],
        small[4],
        small[2],
        small[3],
        up_sum.value,
        flat_sum[:count],
        down_sum.value,
        small[5],
    )


def solution(mesh):
    return jax.shard_map(
        per_device,
        mesh=mesh,
        in_specs=(
            P(("dp", "tensor"), None),
            P(("dp", "tensor"), None),
            P("dp", None),
            P(),
            P(),
            P(None, "tensor"),
            P("tensor"),
            P("tensor", None),
            P(),
            P(),
            P(),
            P(None, "tensor"),
            P("tensor"),
            P("tensor", None),
            P(),
        ),
        out_specs=(
            P(("dp", "tensor"), None),
            P(("dp", "tensor"), None),
            P(),
            P(),
            P(None, "tensor"),
            P("tensor"),
            P("tensor", None),
            P(),
            P(),
            P(),
            P(None, "tensor"),
            P("tensor"),
            P("tensor", None),
            P(),
        ),
        check_vma=False,
    )
```

```python
import functools
import math

import jax
import jax.numpy as jnp
from jax import lax
from jax.experimental import pallas as pl
from jax.experimental.pallas import tpu as pltpu
from jax.sharding import PartitionSpec as P

H = 16
HEAD = 64
EPS = 1e-05
FAR = 1e34
BF = jnp.bfloat16
F32 = jnp.float32
SCALE = 1.0 / math.sqrt(HEAD)
TENSOR = 4


def dot(left, right, left_dim=1, right_dim=0):
    return lax.dot_general(
        left, right, (((left_dim,), (right_dim,)), ((), ())), preferred_element_type=F32
    )


def after(values, *earlier):
    return lax.optimization_barrier((values,) + earlier)[0]


def swap(value, mask):
    return lax.ppermute(value, "tensor", [(i, i ^ mask) for i in range(TENSOR)])


def dp_swap(value, bit):
    count = lax.axis_size("dp")
    return lax.ppermute(value, "dp", [(i, i ^ (1 << bit)) for i in range(count)])


def dp_bits():
    count = lax.axis_size("dp")
    bits = count.bit_length() - 1
    assert 1 << bits == count
    return bits


def my_bit(bit):
    return (lax.axis_index("dp") >> bit) & 1


def join(mine, got, place):
    return jnp.where(
        place == 0,
        jnp.concatenate([mine, got], axis=0),
        jnp.concatenate([got, mine], axis=0),
    )


def split_kernel(place_ref, keep_ref, got_ref, *out_refs):
    rows = keep_ref.shape[0]
    if len(out_refs) == 1:
        out_refs[0][...] = (keep_ref[...].astype(F32) + got_ref[...].astype(F32)).astype(BF)
        return
    half = rows // 2
    for out, place in zip(out_refs, (1 - place_ref[0], place_ref[0])):
        spot = pl.ds(pl.multiple_of(place * half, half), half)
        out[...] = (keep_ref[spot, :].astype(F32) + got_ref[spot, :].astype(F32)).astype(BF)


def place_kernel(index_ref, *refs):
    rows = refs[0].shape[0]
    for k, ref in enumerate(refs[:-1]):
        spot = index_ref[0] ^ k
        refs[-1][pl.ds(pl.multiple_of(spot * rows, rows), rows), :] = ref[...]


def join_kernel(place_ref, mine_ref, got_ref, out_ref):
    rows = mine_ref.shape[0]
    place = place_ref[0]
    mine = pl.ds(pl.multiple_of(place * rows, rows), rows)
    got = pl.ds(pl.multiple_of((1 - place) * rows, rows), rows)
    out_ref[mine, :] = mine_ref[...].astype(out_ref.dtype)
    out_ref[got, :] = got_ref[...].astype(out_ref.dtype)


class DpSum:
    def __init__(self, name, send, keep, sums, joins, final=None):
        self.name = name
        self.final = final
        self.plan = [("sum", bit) for bit in sums] + [("join", bit) for bit in joins]
        self.exchange(send, keep)

    def exchange(self, send, keep):
        kind, bit = self.plan[0]
        self.keep = keep
        with jax.named_scope(f"{self.name}_{kind}_{bit}"):
            self.got = dp_swap(send, bit)

    def step(self, *earlier):
        kind, bit = self.plan.pop(0)
        got = after(self.got, *earlier)
        rows, cols = self.keep.shape
        if kind == "join":
            last = not self.plan
            place = my_bit(bit).astype(jnp.int32).reshape(1)
            if last and self.final is not None:
                self.value = self.final(place, self.keep, got)
                return self.value[0]
            if rows % 16:
                value = join(self.keep, got, my_bit(bit))
            else:
                (value,) = run(
                    self.name + "_join", join_kernel, [((2 * rows, cols), F32 if last else BF)],
                    [place], [self.keep, got],
                )
            self.value = value
            if not last:
                self.exchange(value, value)
            return value
        following, next_bit = self.plan[0]
        place = my_bit(next_bit).astype(jnp.int32).reshape(1)
        if rows % 32:
            value = (self.keep.astype(F32) + got.astype(F32)).astype(BF)
            out = [value]
            if following == "sum":
                out = [
                    lax.dynamic_slice_in_dim(value, spot * (rows // 2), rows // 2, 0)
                    for spot in (1 - my_bit(next_bit), my_bit(next_bit))
                ]
            self.exchange(out[0], out[-1])
            return out[-1]
        shapes = [((rows // 2, cols), BF)] * 2 if following == "sum" else [((rows, cols), BF)]
        out = run(self.name + "_add", split_kernel, shapes, [place], [self.keep, got])
        self.exchange(out[0], out[-1])
        return out[-1]


def pair_kernel(place_ref, first_ref, first_got, second_ref, second_got, send_ref, keep_ref):
    half = first_ref.shape[0] // 2
    cols = first_ref.shape[1]
    for out, place in ((send_ref, 1 - place_ref[0]), (keep_ref, place_ref[0])):
        spot = pl.ds(pl.multiple_of(place * half, half), half)
        for at, (ref, got) in enumerate(((first_ref, first_got), (second_ref, second_got))):
            total = ref[spot, :].astype(F32) + got[spot, :].astype(F32)
            out[:, at * cols : (at + 1) * cols] = total.astype(BF)


def pair_join_kernel(place_ref, mine_ref, got_ref, first_ref, second_ref):
    rows = mine_ref.shape[0]
    cols = first_ref.shape[1]
    for ref, place in ((mine_ref, place_ref[0]), (got_ref, 1 - place_ref[0])):
        spot = pl.ds(pl.multiple_of(place * rows, rows), rows)
        first_ref[spot, :] = ref[:, :cols]
        second_ref[spot, :] = ref[:, cols:]


def pair_join(place, mine, got):
    rows, cols = mine.shape
    shape = (2 * rows, cols // 2)
    return run("pair_join", pair_join_kernel, [(shape, BF)] * 2, [place], [mine, got])


SMEM = pl.BlockSpec(memory_space=pltpu.SMEM)
VMEM = pl.BlockSpec(memory_space=pltpu.VMEM)


def params(mib):
    return pltpu.CompilerParams(vmem_limit_bytes=mib * 1024 * 1024)


def run(name, body, outs, scalars, arrays, mib=6, far=(), scratch=()):
    n_first = len(scalars)
    n_in = n_first + len(arrays)
    n_refs = n_in + len(outs) + len(scratch)

    def fetching(*refs):
        refs, held, sems = list(refs[:n_refs]), refs[n_refs:-1], refs[-1]
        copies = [
            pltpu.make_async_copy(refs[n_first + at], spot, sems.at[i])
            for i, (at, spot) in enumerate(zip(far, held))
        ]
        for copy in copies:
            copy.start()
        for copy in copies:
            copy.wait()
        for at, spot in zip(far, held):
            refs[n_first + at] = spot
        body(*refs)

    specs = [VMEM] * len(arrays)
    scratch = list(scratch)
    for at in far:
        specs[at] = pl.BlockSpec(memory_space=pl.ANY)
        scratch.append(pltpu.VMEM(arrays[at].shape, arrays[at].dtype))
    if far:
        scratch.append(pltpu.SemaphoreType.DMA((len(far),)))
    return pl.pallas_call(
        fetching if far else body,
        name=name,
        out_shape=[jax.ShapeDtypeStruct(shape, dtype) for shape, dtype in outs],
        in_specs=[SMEM] * len(scalars) + specs,
        out_specs=[VMEM] * len(outs),
        scratch_shapes=scratch,
        compiler_params=params(mib),
        cost_estimate=pl.CostEstimate(flops=1, bytes_accessed=1, transcendentals=0),
    )(*scalars, *arrays)


def normalize(values):
    mean = jnp.mean(values, axis=-1, keepdims=True)
    centred = values - mean
    spread = jnp.mean(centred * centred, axis=-1, keepdims=True)
    inverse = lax.rsqrt(spread + EPS)
    return centred * inverse, inverse


def norm_back(grad, unit, inverse, gain):
    g = grad * gain
    return inverse * (
        g
        - jnp.mean(g, axis=-1, keepdims=True)
        - unit * jnp.mean(g * unit, axis=-1, keepdims=True)
    )


def masked_distance(start_ref, block, rows):
    width = (block + 1) * rows
    query = block * rows + lax.broadcasted_iota(jnp.int32, (rows, width), 0)
    key = lax.broadcasted_iota(jnp.int32, (rows, width), 1)
    start = start_ref[block * rows : (block + 1) * rows, :]
    allowed = (key <= query) & (key >= start)
    return jnp.where(allowed, (query - key).astype(F32), FAR)


def spot_of(k, me, rows):
    return pl.ds(pl.multiple_of((k ^ me) * rows, rows), rows)


def forward_kernel(
    me_ref, slope_ref, start_ref, weight_ref, bias_ref, gain_ref, shift_ref, *refs,
):
    token_refs, refs = refs[:TENSOR], refs[TENSOR:]
    ctx_refs, (full_ref, lse_ref, held, norm_ref, made) = refs[:TENSOR], refs[TENSOR:]
    me = me_ref[0]
    rows = token_refs[0].shape[0]
    heads = weight_ref.shape[1] // (3 * HEAD)
    for k, ref in enumerate(token_refs):
        unit, _ = normalize(ref[...].astype(F32))
        norm = (unit * gain_ref[...] + shift_ref[...]).astype(BF)
        norm_ref[k * rows : (k + 1) * rows, :] = norm
        made_qkv = dot(norm, weight_ref[...]) + bias_ref[...]
        held[spot_of(k, me, rows), :] = made_qkv.astype(BF)
    for block in range(TENSOR):
        width = (block + 1) * rows
        distance = masked_distance(start_ref, block, rows)
        for head in range(heads):
            at = head * 3 * HEAD
            query = held[block * rows : width, at : at + HEAD]
            key = held[:width, at + HEAD : at + 2 * HEAD]
            value = held[:width, at + 2 * HEAD : at + 3 * HEAD]
            scores = dot(query, key, 1, 1) * SCALE - slope_ref[head] * distance
            best = jnp.max(scores, axis=1, keepdims=True)
            weights = jnp.exp(scores - best)
            mass = jnp.sum(weights, axis=1, keepdims=True)
            out = dot(weights.astype(BF), value) / mass
            made[block * rows : width, head * HEAD : (head + 1) * HEAD] = out.astype(BF)
            lse_ref[block * rows : width, head : head + 1] = best + jnp.log(mass)
    for k in range(TENSOR):
        part = made[spot_of(k, me, rows), :]
        ctx_refs[k][...] = part
        full_ref[k * rows : (k + 1) * rows, :] = part


def backward_kernel(first, me_ref, slope_ref, start_ref, lse_ref, held, *refs):
    outer_refs, (grad_ref, outer, keys, values, made) = refs[:TENSOR], refs[TENSOR:]
    me = me_ref[0]
    rows = held.shape[0] // TENSOR
    heads = made.shape[1] // (3 * HEAD)
    for k in range(TENSOR):
        outer[spot_of(k, me, rows), :] = outer_refs[k][...]
    for block in reversed(range(TENSOR)):
        width = (block + 1) * rows
        distance = masked_distance(start_ref, block, rows)
        for head in range(heads):
            at = head * 3 * HEAD
            cols = slice(head * HEAD, (head + 1) * HEAD)
            own = first + head
            took = own * 3 * HEAD
            query = held[block * rows : width, took : took + HEAD]
            key = held[:width, took + HEAD : took + 2 * HEAD]
            value = held[:width, took + 2 * HEAD : took + 3 * HEAD]
            grad = outer[block * rows : width, own * HEAD : (own + 1) * HEAD]
            lse = lse_ref[block * rows : width, own : own + 1]
            scores = dot(query, key, 1, 1) * SCALE - slope_ref[own] * distance
            probs = jnp.exp(scores - lse)
            prob_grad = dot(grad, value, 1, 1)
            delta = jnp.sum(probs * prob_grad, axis=1, keepdims=True)
            score_grad = (probs * (prob_grad - delta)).astype(BF)
            key_part = dot(score_grad, query, 0, 0)
            value_part = dot(probs.astype(BF), grad, 0, 0)
            if block == TENSOR - 1:
                keys[:width, cols] = key_part
                values[:width, cols] = value_part
            else:
                keys[:width, cols] += key_part
                values[:width, cols] += value_part
            made[block * rows : width, at : at + HEAD] = (dot(score_grad, key) * SCALE).astype(BF)
    for head in range(heads):
        at = head * 3 * HEAD
        cols = slice(head * HEAD, (head + 1) * HEAD)
        made[:, at + HEAD : at + 2 * HEAD] = (keys[:, cols] * SCALE).astype(BF)
        made[:, at + 2 * HEAD : at + 3 * HEAD] = values[:, cols].astype(BF)
    for k in range(TENSOR):
        grad_ref[k * rows : (k + 1) * rows, :] = made[spot_of(k, me, rows), :]


def attention(me, slopes, start, weight, bias, gain, shift, tokens):
    rows, model = tokens[0].shape
    width = weight.shape[1]
    total = rows * TENSOR
    wide = width // 3
    out = run(
        "attention_forward",
        forward_kernel,
        [((rows, wide), BF)] * TENSOR
        + [
            ((total, wide), BF),
            ((total, wide // HEAD), F32),
            ((total, width), BF),
            ((total, model), BF),
        ],
        [me, slopes],
        [start, weight, bias[None], gain[None], shift[None], *tokens],
        22,
        far=(1, 5, 6, 7, 8),
        scratch=[pltpu.VMEM((total, wide), BF)],
    )
    return out[:TENSOR], *out[TENSOR:]


def attention_back(me, slopes, start, lse, held, outer, first, heads):
    total, width = held.shape
    made = heads * 3 * HEAD
    return run(
        "attention_backward",
        functools.partial(backward_kernel, first),
        [((total, made), BF)],
        [me, slopes],
        [start, lse, held, *outer],
        28,
        far=(2, 3, 4, 5, 6),
        scratch=[
            pltpu.VMEM((total, width // 3), BF),
            pltpu.VMEM((total, heads * HEAD), F32),
            pltpu.VMEM((total, heads * HEAD), F32),
            pltpu.VMEM((total, made), BF),
        ],
    )[0]


def norm2_back_kernel(
    part_ref, beside_ref, across_ref, unit_ref, inverse_ref, gain_ref, cot_ref, *refs
):
    weight_refs, (resid_ref, low_ref, sums_ref), ctx_refs = (
        refs[:TENSOR],
        refs[TENSOR : TENSOR + 3],
        refs[TENSOR + 3 :],
    )
    rows = beside_ref.shape[0]
    grad = (
        part_ref[:rows, :].astype(F32)
        + beside_ref[...].astype(F32)
        + across_ref[...].astype(F32)
    )
    unit = unit_ref[...]
    resid = cot_ref[...].astype(F32) + norm_back(grad, unit, inverse_ref[...], gain_ref[...])
    low = resid.astype(BF)
    resid_ref[...] = resid
    low_ref[...] = low
    sums_ref[0:1, :] = jnp.sum(grad * unit, axis=0, keepdims=True)
    sums_ref[1:2, :] = jnp.sum(grad, axis=0, keepdims=True)
    sums_ref[2:3, :] = jnp.sum(low.astype(F32), axis=0, keepdims=True)
    sums_ref[3:4, :] = jnp.sum(cot_ref[...].astype(F32), axis=0, keepdims=True)
    for ctx, weight in zip(ctx_refs, weight_refs):
        ctx[...] = dot(low, weight[...], 1, 1).astype(BF)


def norm2_back(part, beside, across, unit, inverse, gain, cot, weights):
    rows, width = beside.shape
    out = run(
        "norm2_back",
        norm2_back_kernel,
        [((rows, width), F32), ((rows, width), BF), ((4, width), F32)]
        + [((rows, weight.shape[0]), BF) for weight in weights],
        [],
        [part, beside, across, unit, inverse, gain[None], cot, *weights],
        10,
        far=(1, 2, 6, 7, 8, 9, 10),
    )
    return out[0], out[1], out[2], out[3:]


def norm1_part_kernel(first_ref, second_ref, weight_ref, *refs):
    token_refs, part_refs, sums_ref = refs[:TENSOR], refs[TENSOR:-1], refs[-1]
    rows = token_refs[0].shape[0]
    cut = first_ref.shape[1]
    gain_sum, shift_sum = 0.0, 0.0
    for k, (tokens, part) in enumerate(zip(token_refs, part_refs)):
        spot = slice(k * rows, (k + 1) * rows)
        grad = dot(first_ref[spot, :], weight_ref[:, :cut], 1, 1)
        grad += dot(second_ref[spot, :], weight_ref[:, cut:], 1, 1)
        part[...] = grad.astype(BF)
        unit, _ = normalize(tokens[...].astype(F32))
        gain_sum += jnp.sum(grad * unit, axis=0, keepdims=True)
        shift_sum += jnp.sum(grad, axis=0, keepdims=True)
    sums_ref[0:1, :] = gain_sum
    sums_ref[1:2, :] = shift_sum


def norm1_back_kernel(*refs):
    part_refs, (tokens_ref, gain_ref, resid_ref, grad_ref) = refs[:TENSOR], refs[TENSOR:]
    grad = part_refs[0][...].astype(F32)
    for ref in part_refs[1:]:
        grad += ref[...].astype(F32)
    unit, inverse = normalize(tokens_ref[...].astype(F32))
    grad_ref[...] = (
        resid_ref[...] + norm_back(grad, unit, inverse, gain_ref[...])
    ).astype(BF)


def norm1_back(parts, tokens, gain, resid):
    return run(
        "norm1_back",
        norm1_back_kernel,
        [(tokens.shape, BF)],
        [],
        [*parts, tokens, gain[None], resid],
        12,
        far=(0, 1, 2, 3, 4, 6),
    )[0]


def dense_kernel(tokens_ref, bias_ref, gain_ref, shift_ref, *refs):
    heads_refs, refs = refs[:TENSOR], refs[TENSOR:]
    weight_refs, (resid_ref, norm_ref, unit_ref, inverse_ref) = refs[:TENSOR], refs[TENSOR:]
    total = dot(heads_refs[0][...], weight_refs[0][...])
    for k in range(1, TENSOR):
        total += dot(heads_refs[k][...], weight_refs[k][...])
    resid = tokens_ref[...].astype(F32) + (total + bias_ref[...])
    unit, inverse = normalize(resid)
    resid_ref[...] = resid
    unit_ref[...] = unit
    inverse_ref[...] = inverse
    norm_ref[...] = (unit * gain_ref[...] + shift_ref[...]).astype(BF)


def dense_norm(tokens, bias, gain, shift, mixed, weights):
    rows, width = tokens.shape
    return run(
        "dense_norm",
        dense_kernel,
        [((rows, width), F32), ((rows, width), BF), ((rows, width), F32), ((rows, 1), F32)],
        [],
        [tokens, bias[None], gain[None], shift[None], *mixed, *weights],
        10,
        far=(0, 4, 5, 6, 7, 8, 9, 10, 11),
    )


ROOT = math.sqrt(2.0 / math.pi)
CUBE = 0.044715


def feed_kernel(first_ref, second_ref, weight_ref, bias_ref, grad_ref, act_ref, pre_ref):
    rows = first_ref.shape[0]
    wide = min(256, weight_ref.shape[1])
    for i, ref in enumerate((first_ref, second_ref)):
        part = slice(i * rows, (i + 1) * rows)
        for at in range(0, weight_ref.shape[1], wide):
            cols = slice(at, at + wide)
            u = dot(ref[...], weight_ref[:, cols]) + bias_ref[:, cols]
            square = u * u
            bent = jnp.tanh(ROOT * (u + CUBE * (square * u)))
            half = 0.5 * (1.0 + bent)
            act_ref[part, cols] = (u * half).astype(BF)
            slope = half + 0.5 * u * (1.0 - bent * bent) * (ROOT + (3.0 * CUBE * ROOT) * square)
            pre_ref[part, cols] = (grad_ref[part, cols] * slope).astype(BF)


def feed(first, second, weight, bias, act_grad):
    shape = (2 * first.shape[0], weight.shape[1])
    return run(
        "feed_forward",
        feed_kernel,
        [(shape, BF)] * 2,
        [],
        [first, second, weight, bias[None], act_grad],
        12,
        far=(0, 1, 2),
    )


def rows_kernel(first_ref, second_ref, weight_ref, out_ref):
    rows = first_ref.shape[0]
    out_ref[:rows, :] = dot(first_ref[...], weight_ref[...], 1, 1)
    out_ref[rows:, :] = dot(second_ref[...], weight_ref[...], 1, 1)


def act_gradient(first, second, weight):
    shape = (2 * first.shape[0], weight.shape[0])
    return run("act_grad", rows_kernel, [(shape, F32)], [], [first, second, weight], 8)[0]


def part_kernel(side, value_ref, weight_ref, keep_ref, send_ref):
    rows = keep_ref.shape[0]
    keep_ref[...] = dot(value_ref[:rows, :], weight_ref[...], 1, side).astype(BF)
    send_ref[...] = dot(value_ref[rows:, :], weight_ref[...], 1, side).astype(BF)


def partial_rows(name, value, weight, side):
    shape = (value.shape[0] // 2, weight.shape[1 - side])
    body = functools.partial(part_kernel, side)
    return run(name, body, [(shape, BF)] * 2, [], [value, weight], 8)


def row_chunks(refs, rows):
    out = []
    for ref in refs:
        for at in range(0, ref.shape[0], rows):
            out.append((ref, slice(at, at + rows)))
    return out


def gradient_kernel(pieces, n_left, n_right, n_base, sums, places_ref, *refs):
    left, refs = refs[:n_left], refs[n_left:]
    right, refs = refs[:n_right], refs[n_right:]
    base, refs = refs[:n_base], refs[n_base:]
    rows = min(ref.shape[0] for ref in left + right)
    left = row_chunks(left, rows)
    right = row_chunks(right, rows)
    if pieces is None:
        height = refs[0].shape[0]
        pieces = [(0, height, None)]
    out = 0
    for first, height, bit in pieces:
        half = height if bit is None else height // 2
        step = min(256, half)
        for place in (None,) if bit is None else (1 - places_ref[bit], places_ref[bit]):
            for at in range(0, half, step):
                if place is None:
                    spot = pl.ds(first + at, step)
                else:
                    spot = pl.ds(pl.multiple_of(first + place * half + at, step), step)
                total = base[0][spot, :] if base else None
                for (l_ref, l_rows), (r_ref, r_rows) in zip(left, right):
                    term = dot(l_ref[l_rows, spot], r_ref[r_rows, :], 0, 0)
                    total = term if total is None else total + term
                refs[out][at : at + step, :] = total.astype(refs[out].dtype)
            out += 1
    if sums:
        total = None
        for ref, part in right:
            term = jnp.sum(ref[part, :].astype(F32), axis=0, keepdims=True)
            total = term if total is None else total + term
        refs[out][...] = total


def gradient(name, places, left, right, pieces, base=(), sums=False, mib=12):
    height, cols = left[0].shape[1], right[0].shape[1]
    if pieces is None:
        outs = [((height, cols), F32)]
    else:
        outs = [((rows // 2, cols), BF) for _, rows, _ in pieces for _ in range(2)]
    if sums:
        outs.append(((1, cols), F32))
    body = functools.partial(
        gradient_kernel, pieces, len(left), len(right), len(base), sums
    )
    return run(name, body, outs, [places], [*left, *right, *base], mib)


def output_kernel(resid_ref, bias_ref, *refs):
    mixed = refs[0][...].astype(F32)
    for ref in refs[1:-1]:
        mixed += ref[...].astype(F32)
    refs[-1][...] = (resid_ref[...] + (mixed + bias_ref[...])).astype(BF)


TAIL = 64


def late_kernel(bit, places_ref, norm_ref, first_ref, second_ref, context_ref, small_ref, *refs):
    resid_refs, (send_ref, keep_ref) = refs[:TENSOR], refs[TENSOR:]
    rows = resid_refs[0].shape[0]
    half = send_ref.shape[0] - TAIL
    cut = first_ref.shape[1]
    step = min(256, half)
    for out, place in ((send_ref, 1 - places_ref[bit]), (keep_ref, places_ref[bit])):
        for at in range(0, half, step):
            spot = pl.ds(pl.multiple_of(place * half + at, step), step)
            norm = norm_ref[:, spot]
            out[at : at + step, :cut] = dot(norm, first_ref[...], 0, 0).astype(BF)
            out[at : at + step, cut : 2 * cut] = dot(norm, second_ref[...], 0, 0).astype(BF)
            total = None
            for k, resid in enumerate(resid_refs):
                term = dot(resid[:, spot], context_ref[k * rows : (k + 1) * rows, :], 0, 0)
                total = term if total is None else total + term
            out[at : at + step, 2 * cut :] = total.astype(BF)
    width = send_ref.shape[1]
    last = jnp.concatenate(
        [
            jnp.sum(first_ref[...].astype(F32), axis=0, keepdims=True),
            jnp.sum(second_ref[...].astype(F32), axis=0, keepdims=True),
            jnp.zeros((1, width - 2 * cut), F32),
        ],
        axis=1,
    )
    count = small_ref.shape[0]
    tail = jnp.concatenate(
        [small_ref[...], last, jnp.zeros((TAIL - count - 1, width), F32)], axis=0
    ).astype(BF)
    send_ref[half:, :] = tail
    keep_ref[half:, :] = tail


def both_kernel(bit, places_ref, norm_ref, grad_ref, context_ref, small_ref, *refs):
    cut = grad_ref.shape[1] // 2
    first_ref, second_ref = grad_ref.at[:, :cut], grad_ref.at[:, cut:]
    resid_refs, refs = refs[:TENSOR], refs[TENSOR:]
    weight_ref, refs = refs[0], refs[1:]
    token_refs, refs = refs[:TENSOR], refs[TENSOR:]
    (send_ref, keep_ref), refs = refs[:2], refs[2:]
    part_refs, sums_ref = refs[:TENSOR], refs[TENSOR]
    norm1_part_kernel(
        first_ref, second_ref, weight_ref, *token_refs, *part_refs, sums_ref.at[0:2, :]
    )
    sums_ref[2:, :] = small_ref[...]
    late_kernel(
        bit, places_ref, norm_ref, first_ref, second_ref, context_ref, sums_ref, *resid_refs,
        send_ref, keep_ref,
    )


def late_gradient(places, bit, norm, grad, context, small, resid, weight, tokens):
    model = norm.shape[1]
    cols = grad.shape[1] + context.shape[1]
    shape = (model // 2 + TAIL, cols)
    return run(
        "qkv_dense",
        functools.partial(both_kernel, bit),
        [(shape, BF)] * 2 + [(tokens[0].shape, BF)] * TENSOR,
        [places],
        [norm, grad, context, small, *resid, weight, *tokens],
        22,
        far=(0, 2, 4, 5, 6, 7, 8, 9, 10, 11, 12),
        scratch=[pltpu.VMEM((2 + small.shape[0], model), F32)],
    )


def late_join_kernel(place_ref, mine_ref, got_ref, qkv_ref, dense_ref):
    rows = mine_ref.shape[0]
    cut = qkv_ref.shape[1]
    for ref, place in ((mine_ref, place_ref[0]), (got_ref, 1 - place_ref[0])):
        spot = pl.ds(pl.multiple_of(place * rows, rows), rows)
        qkv_ref[spot, :] = ref[:, :cut].astype(F32)
        dense_ref[:, spot] = ref[:, cut:].astype(F32).T


def unmix_kernel(place_ref, mine_ref, got_ref, late_ref, small_ref):
    rows = mine_ref.shape[0]
    rest = rows - TAIL

    def put(low_ref, high_ref):
        late_ref[:rows, :] = low_ref[...]
        late_ref[rows:, :] = high_ref[:rest, :]
        small_ref[...] = high_ref[rest:, :].astype(F32)

    @pl.when(place_ref[0] == 0)
    def _():
        put(mine_ref, got_ref)

    @pl.when(place_ref[0] != 0)
    def _():
        put(got_ref, mine_ref)


def unmix(place, mine, got):
    rows, cols = mine.shape
    return run(
        "qkv_dense_small_join",
        unmix_kernel,
        [((2 * rows - TAIL, cols), BF), ((TAIL, cols), F32)],
        [place],
        [mine, got],
    )


def late_join(cut, place, mine, got):
    rows, cols = mine.shape
    return run(
        "qkv_dense_join",
        late_join_kernel,
        [((2 * rows, cut), F32), ((cols - cut, 2 * rows), F32)],
        [place],
        [mine, got],
    )


def add_kernel(first_ref, second_ref, out_ref):
    out_ref[...] = (first_ref[...].astype(F32) + second_ref[...].astype(F32)).astype(BF)


def add_rows(first, second):
    return run("add_rows", add_kernel, [(first.shape, BF)], [], [first, second])[0]


def per_device(
    tokens,
    cotangent,
    seq_lengths,
    ln1_gain,
    ln1_bias,
    qkv_weight,
    qv_bias,
    dense_weight,
    dense_bias,
    ln2_gain,
    ln2_bias,
    up_weight,
    up_bias,
    down_weight,
    down_bias,
):
    rows = tokens.shape[0]
    total = rows * TENSOR
    heads = qkv_weight.shape[1] // (3 * HEAD)
    wide = heads * HEAD
    bits = dp_bits()
    x_first = list(range(bits))
    mixed_order = x_first[1::-1] + x_first[2:]
    rank = lax.axis_index("tensor")
    me = rank.astype(jnp.int32).reshape(1)
    slopes = jnp.exp2(
        -8.0 * ((rank * heads + jnp.arange(heads, dtype=jnp.int32)).astype(F32) + 1.0) / H
    )
    ends = jnp.cumsum(seq_lengths[0])
    positions = jnp.arange(total, dtype=jnp.int32)
    start = jnp.max(
        jnp.where(ends[None, :] <= positions[:, None], ends[None, :], 0), axis=1, keepdims=True
    )
    gain1, shift1 = ln1_gain.astype(F32), ln1_bias.astype(F32)
    gain2, shift2 = ln2_gain.astype(F32), ln2_bias.astype(F32)

    places = jnp.stack([my_bit(bit) for bit in range(bits)]).astype(jnp.int32)
    shares = 1 << min(bits, 2)
    piece = dense_weight.shape[0] // shares
    low_index = (lax.axis_index("dp") & (shares - 1)).astype(jnp.int32)
    part = swap(lax.dynamic_slice_in_dim(dense_weight, low_index * piece, piece, 0), 2)
    tokens_2 = swap(tokens, 2)
    tokens_1 = swap(tokens, 1)
    pair = qv_bias.astype(F32).reshape(heads, 2, HEAD)
    bias_full = jnp.stack([pair[:, 0], jnp.zeros_like(pair[:, 0]), pair[:, 1]], axis=1).reshape(
        3 * wide
    )
    cot_1 = swap(cotangent, 1)
    dense_1 = swap(dense_weight, 1)
    tokens_2, tokens_1, cot_1, dense_1, part, start, bias_full, slopes = lax.optimization_barrier(
        (tokens_2, tokens_1, cot_1, dense_1, part, start, bias_full, slopes)
    )
    tokens_3 = swap(tokens_2, 1)
    cot_2 = swap(after(cotangent, tokens_2), 2)
    count = lax.axis_size("dp")
    shared_parts = [part] + [
        lax.ppermute(part, "dp", [(i, i ^ k) for i in range(count)]) for k in range(1, shares)
    ]
    all_tokens = (tokens, tokens_1, tokens_2, tokens_3)
    blocks, context, lse, held, norm1 = attention(
        me, slopes, start, qkv_weight, bias_full, gain1, shift1, all_tokens
    )
    mixed_3 = swap(blocks[3], 3)
    mixed_2 = swap(blocks[2], 2)
    mixed_1 = swap(blocks[1], 1)
    *shared_parts, cot_2, _ = lax.optimization_barrier((*shared_parts, cot_2, context))
    (dense_2,) = run(
        "dense_rows",
        place_kernel,
        [(dense_weight.shape, BF)],
        [low_index.reshape(1)],
        list(shared_parts),
    )
    dense_3 = swap(dense_2, 1)
    dense = [dense_weight, dense_1, dense_2, dense_3]
    cot_3 = swap(cot_2, 1)
    act_grad_a = act_gradient(after(cotangent, dense_2), cot_1, down_weight)
    mixed = lax.optimization_barrier((blocks[0], mixed_1, mixed_2, mixed_3, act_grad_a))[:TENSOR]
    resid, norm2_0, unit2, inverse2 = dense_norm(
        tokens, dense_bias.astype(F32), gain2, shift2, mixed, dense
    )

    norm2_2 = swap(norm2_0, 2)
    norm2_1 = swap(norm2_0, 1)
    up_shift = up_bias.astype(F32)
    act_a, pre_a = feed(norm2_0, norm2_1, up_weight, up_shift, act_grad_a)
    act_grad_b = act_gradient(after(cot_2, act_a), cot_3, down_weight)
    (down_a,) = gradient("down_a", places, [act_a], [cotangent, cot_1], None)
    norm2_2 = lax.optimization_barrier((norm2_2, act_grad_b, down_a))[0]
    norm2_3 = swap(norm2_2, 1)
    act_b, pre_b = feed(norm2_2, norm2_3, up_weight, up_shift, act_grad_b)

    units = down_weight.shape[0]
    down_send, down_keep = gradient(
        "down", places, [act_b], [cot_2, cot_3], [(0, units, x_first[0])], [down_a]
    )
    down_sum = DpSum("down", down_send, down_keep, x_first[:2], [])
    keep_b, send_b = partial_rows("norm2_part_b", after(pre_b, down_keep), up_weight, 1)
    beside_b = swap(send_b, 1)
    model = up_weight.shape[0]
    norms = [norm2_0, norm2_1, norm2_2, norm2_3]
    up_send, up_keep, up_shift_grad = gradient(
        "up", places, norms, [pre_a, after(pre_b, keep_b)], [(0, model, mixed_order[0])], sums=True
    )
    across = swap(add_rows(keep_b, after(beside_b, up_keep)), 2)
    up_sum = DpSum("up", up_send, up_keep, mixed_order[:2], [])
    keep_a, send_a = partial_rows("norm2_part_a", after(pre_a, up_keep), up_weight, 1)
    beside_a = swap(send_a, 1)
    out_keep_b, out_send_b = partial_rows("out_part_b", after(act_b, keep_a), down_weight, 0)
    out_keep_a, out_send_a = partial_rows("out_part_a", after(act_a, keep_a), down_weight, 0)
    across = lax.optimization_barrier((across, out_keep_a, out_keep_b))[0]
    resid_grad, resid_low, sums2, ctx_grad = norm2_back(
        keep_a, beside_a, across, unit2, inverse2, gain2, cotangent, dense
    )

    outer_3 = swap(ctx_grad[3], 3)
    outer_2 = swap(ctx_grad[2], 2)
    outer_1 = swap(ctx_grad[1], 1)
    resid_1 = swap(resid_low, 1)
    outer = lax.optimization_barrier((ctx_grad[0], outer_1, outer_2, outer_3))
    last = down_sum.step(*outer)
    last = up_sum.step(last)
    outer = lax.optimization_barrier((*outer, last))[:TENSOR]
    resid_2 = swap(after(resid_low, *outer), 2)
    qkv_grad = attention_back(me, slopes, start, lse, held, outer, 0, heads)
    late_bits = x_first[2:]
    place = my_bit(late_bits[0]).astype(jnp.int32).reshape(1)
    down_got, up_got, _ = lax.optimization_barrier((down_sum.got, up_sum.got, qkv_grad))
    quarter = down_sum.keep.shape[0]
    pair_send, pair_keep = run(
        "pair_add",
        pair_kernel,
        [((quarter // 2, 2 * model), BF)] * 2,
        [place],
        [down_sum.keep, down_got, up_sum.keep, up_got],
    )
    pair_sum = DpSum("pair", pair_send, pair_keep, late_bits, late_bits[::-1], pair_join)
    qkv_grad, resid_2, _ = lax.optimization_barrier((qkv_grad, resid_2, pair_keep))
    resid_3 = swap(resid_2, 1)
    units = up_shift_grad.shape[1]
    up_rows = jnp.pad(up_shift_grad, ((0, 0), (0, -units % model))).reshape(-1, model)
    small = jnp.concatenate([sums2, up_rows], axis=0)
    late_send, late_keep, *parts = late_gradient(
        places, x_first[0], norm1, qkv_grad, context, small,
        [resid_low, resid_1, resid_2, resid_3], qkv_weight, all_tokens,
    )
    late_sum = DpSum("late", late_send, late_keep, x_first, x_first[:0:-1], unmix)
    last = pair_sum.step(late_keep)
    part_3 = swap(after(parts[3], last), 3)
    part_2 = swap(after(parts[2], last), 2)
    part_1 = swap(after(parts[1], last), 1)
    out_1 = swap(after(out_send_a, part_1), 1)

    last = late_sum.step(out_1)
    while pair_sum.plan:
        last = pair_sum.step(last)
    down_rest, up_rest = pair_sum.value
    down_sum = DpSum("down", down_rest, down_rest, [], x_first[1::-1])
    up_sum = DpSum("up", up_rest, up_rest, [], mixed_order[1::-1])
    last = late_sum.step(down_rest)
    parts = lax.optimization_barrier((parts[0], part_1, part_2, part_3, last))[:TENSOR]
    grad_tokens = norm1_back(parts, tokens, gain1, resid_grad)
    out_3 = swap(after(out_send_b, grad_tokens), 3)
    out_2 = swap(after(out_keep_b, grad_tokens), 2)

    last = up_sum.step(grad_tokens)
    for _ in range(bits - 2):
        last = late_sum.step(last)
    last = down_sum.step(last)
    mixed = lax.optimization_barrier((out_keep_a, out_1, out_2, out_3, last))[:TENSOR]
    (output,) = run(
        "output",
        output_kernel,
        [(resid.shape, BF)],
        [],
        [resid, down_bias.astype(F32)[None], *mixed],
        12,
        far=(0, 2, 3, 4, 5),
    )
    last = late_sum.step(output)
    last = down_sum.step(last)
    while late_sum.plan:
        last = late_sum.step(last)
    late_rest, small = late_sum.value
    late_sum = DpSum(
        "late", late_rest, late_rest, [], x_first[:1], functools.partial(late_join, 3 * wide)
    )
    shared = small[:6]
    shared = shared + swap(shared, 1)
    shared = shared + swap(shared, 2)
    last = up_sum.step(shared)
    late_sum.step(last)
    count = up_rows.shape[0]
    up_total = small[6 : 6 + count].reshape(-1)[:units]
    slot_sums = small[6 + count, : 3 * wide].reshape(heads, 3, HEAD)
    grad_qv_bias = jnp.stack([slot_sums[:, 0], slot_sums[:, 2]], axis=1).reshape(2 * wide)
    return (
        output,
        grad_tokens,
        shared[0],
        shared[1],
        late_sum.value[0],
        grad_qv_bias,
        late_sum.value[1],
        shared[4],
        shared[2],
        shared[3],
        up_sum.value,
        up_total,
        down_sum.value,
        shared[5],
    )


def solution(mesh):
    return jax.shard_map(
        per_device,
        mesh=mesh,
        in_specs=(
            P(("dp", "tensor"), None),
            P(("dp", "tensor"), None),
            P("dp", None),
            P(),
            P(),
            P(None, "tensor"),
            P("tensor"),
            P("tensor", None),
            P(),
            P(),
            P(),
            P(None, "tensor"),
            P("tensor"),
            P("tensor", None),
            P(),
        ),
        out_specs=(
            P(("dp", "tensor"), None),
            P(("dp", "tensor"), None),
            P(),
            P(),
            P(None, "tensor"),
            P("tensor"),
            P("tensor", None),
            P(),
            P(),
            P(),
            P(None, "tensor"),
            P("tensor"),
            P("tensor", None),
            P(),
        ),
        check_vma=False,
    )
```

```python
import functools
import math

import jax
import jax.numpy as jnp
from jax import lax
from jax.experimental import pallas as pl
from jax.experimental.pallas import tpu as pltpu
from jax.sharding import PartitionSpec as P

H = 16
HEAD = 64
EPS = 1e-05
FAR = 1e34
BF = jnp.bfloat16
F32 = jnp.float32
SCALE = 1.0 / math.sqrt(HEAD)
TENSOR = 4


def dot(left, right, left_dim=1, right_dim=0):
    return lax.dot_general(
        left, right, (((left_dim,), (right_dim,)), ((), ())), preferred_element_type=F32
    )


def after(values, *earlier):
    return lax.optimization_barrier((values,) + earlier)[0]


def swap(value, mask):
    return lax.ppermute(value, "tensor", [(i, i ^ mask) for i in range(TENSOR)])


def dp_swap(value, bit):
    count = lax.axis_size("dp")
    return lax.ppermute(value, "dp", [(i, i ^ (1 << bit)) for i in range(count)])


def dp_bits():
    count = lax.axis_size("dp")
    bits = count.bit_length() - 1
    assert 1 << bits == count
    return bits


def my_bit(bit):
    return (lax.axis_index("dp") >> bit) & 1


def join(mine, got, place):
    return jnp.where(
        place == 0,
        jnp.concatenate([mine, got], axis=0),
        jnp.concatenate([got, mine], axis=0),
    )


def split_kernel(place_ref, keep_ref, got_ref, *out_refs):
    rows = keep_ref.shape[0]
    if len(out_refs) == 1:
        out_refs[0][...] = (keep_ref[...].astype(F32) + got_ref[...].astype(F32)).astype(BF)
        return
    half = rows // 2
    for out, place in zip(out_refs, (1 - place_ref[0], place_ref[0])):
        spot = pl.ds(pl.multiple_of(place * half, half), half)
        out[...] = (keep_ref[spot, :].astype(F32) + got_ref[spot, :].astype(F32)).astype(BF)


def place_kernel(index_ref, *refs):
    rows = refs[0].shape[0]
    for k, ref in enumerate(refs[:-1]):
        spot = index_ref[0] ^ k
        refs[-1][pl.ds(pl.multiple_of(spot * rows, rows), rows), :] = ref[...]


def join_kernel(place_ref, mine_ref, got_ref, out_ref):
    rows = mine_ref.shape[0]
    place = place_ref[0]
    mine = pl.ds(pl.multiple_of(place * rows, rows), rows)
    got = pl.ds(pl.multiple_of((1 - place) * rows, rows), rows)
    out_ref[mine, :] = mine_ref[...].astype(out_ref.dtype)
    out_ref[got, :] = got_ref[...].astype(out_ref.dtype)


class DpSum:
    def __init__(self, name, send, keep, sums, joins, final=None):
        self.name = name
        self.final = final
        self.plan = [("sum", bit) for bit in sums] + [("join", bit) for bit in joins]
        self.exchange(send, keep)

    def exchange(self, send, keep):
        kind, bit = self.plan[0]
        self.keep = keep
        with jax.named_scope(f"{self.name}_{kind}_{bit}"):
            self.got = dp_swap(send, bit)

    def step(self, *earlier):
        kind, bit = self.plan.pop(0)
        got = after(self.got, *earlier)
        rows, cols = self.keep.shape
        if kind == "join":
            last = not self.plan
            place = my_bit(bit).astype(jnp.int32).reshape(1)
            if last and self.final is not None:
                self.value = self.final(place, self.keep, got)
                return self.value[0]
            if rows % 16:
                value = join(self.keep, got, my_bit(bit))
            else:
                (value,) = run(
                    self.name + "_join", join_kernel, [((2 * rows, cols), F32 if last else BF)],
                    [place], [self.keep, got],
                )
            self.value = value
            if not last:
                self.exchange(value, value)
            return value
        following, next_bit = self.plan[0]
        place = my_bit(next_bit).astype(jnp.int32).reshape(1)
        if rows % 32:
            value = (self.keep.astype(F32) + got.astype(F32)).astype(BF)
            out = [value]
            if following == "sum":
                out = [
                    lax.dynamic_slice_in_dim(value, spot * (rows // 2), rows // 2, 0)
                    for spot in (1 - my_bit(next_bit), my_bit(next_bit))
                ]
            self.exchange(out[0], out[-1])
            return out[-1]
        shapes = [((rows // 2, cols), BF)] * 2 if following == "sum" else [((rows, cols), BF)]
        out = run(self.name + "_add", split_kernel, shapes, [place], [self.keep, got])
        self.exchange(out[0], out[-1])
        return out[-1]


def pair_kernel(place_ref, first_ref, first_got, second_ref, second_got, send_ref, keep_ref):
    half = first_ref.shape[0] // 2
    cols = first_ref.shape[1]
    for out, place in ((send_ref, 1 - place_ref[0]), (keep_ref, place_ref[0])):
        spot = pl.ds(pl.multiple_of(place * half, half), half)
        for at, (ref, got) in enumerate(((first_ref, first_got), (second_ref, second_got))):
            total = ref[spot, :].astype(F32) + got[spot, :].astype(F32)
            out[:, at * cols : (at + 1) * cols] = total.astype(BF)


def pair_join_kernel(place_ref, mine_ref, got_ref, first_ref, second_ref):
    rows = mine_ref.shape[0]
    cols = first_ref.shape[1]
    for ref, place in ((mine_ref, place_ref[0]), (got_ref, 1 - place_ref[0])):
        spot = pl.ds(pl.multiple_of(place * rows, rows), rows)
        first_ref[spot, :] = ref[:, :cols]
        second_ref[spot, :] = ref[:, cols:]


def pair_join(place, mine, got):
    rows, cols = mine.shape
    shape = (2 * rows, cols // 2)
    return run("pair_join", pair_join_kernel, [(shape, BF)] * 2, [place], [mine, got])


SMEM = pl.BlockSpec(memory_space=pltpu.SMEM)
VMEM = pl.BlockSpec(memory_space=pltpu.VMEM)


def params(mib):
    return pltpu.CompilerParams(vmem_limit_bytes=mib * 1024 * 1024)


def run(name, body, outs, scalars, arrays, mib=6, far=(), scratch=()):
    n_first = len(scalars)
    n_in = n_first + len(arrays)
    n_refs = n_in + len(outs) + len(scratch)

    def fetching(*refs):
        refs, held, sems = list(refs[:n_refs]), refs[n_refs:-1], refs[-1]
        copies = [
            pltpu.make_async_copy(refs[n_first + at], spot, sems.at[i])
            for i, (at, spot) in enumerate(zip(far, held))
        ]
        for copy in copies:
            copy.start()
        for copy in copies:
            copy.wait()
        for at, spot in zip(far, held):
            refs[n_first + at] = spot
        body(*refs)

    specs = [VMEM] * len(arrays)
    scratch = list(scratch)
    for at in far:
        specs[at] = pl.BlockSpec(memory_space=pl.ANY)
        scratch.append(pltpu.VMEM(arrays[at].shape, arrays[at].dtype))
    if far:
        scratch.append(pltpu.SemaphoreType.DMA((len(far),)))
    return pl.pallas_call(
        fetching if far else body,
        name=name,
        out_shape=[jax.ShapeDtypeStruct(shape, dtype) for shape, dtype in outs],
        in_specs=[SMEM] * len(scalars) + specs,
        out_specs=[VMEM] * len(outs),
        scratch_shapes=scratch,
        compiler_params=params(mib),
        cost_estimate=pl.CostEstimate(flops=1, bytes_accessed=1, transcendentals=0),
    )(*scalars, *arrays)


def normalize(values):
    mean = jnp.mean(values, axis=-1, keepdims=True)
    centred = values - mean
    spread = jnp.mean(centred * centred, axis=-1, keepdims=True)
    inverse = lax.rsqrt(spread + EPS)
    return centred * inverse, inverse


def norm_back(grad, unit, inverse, gain):
    g = grad * gain
    return inverse * (
        g
        - jnp.mean(g, axis=-1, keepdims=True)
        - unit * jnp.mean(g * unit, axis=-1, keepdims=True)
    )


def masked_distance(start_ref, block, rows):
    width = (block + 1) * rows
    query = block * rows + lax.broadcasted_iota(jnp.int32, (rows, width), 0)
    key = lax.broadcasted_iota(jnp.int32, (rows, width), 1)
    start = start_ref[block * rows : (block + 1) * rows, :]
    allowed = (key <= query) & (key >= start)
    return jnp.where(allowed, (query - key).astype(F32), FAR)


def spot_of(k, me, rows):
    return pl.ds(pl.multiple_of((k ^ me) * rows, rows), rows)


def forward_kernel(
    me_ref, slope_ref, start_ref, weight_ref, bias_ref, gain_ref, shift_ref, *refs,
):
    token_refs, refs = refs[:TENSOR], refs[TENSOR:]
    ctx_refs, (full_ref, lse_ref, held, norm_ref, made) = refs[:TENSOR], refs[TENSOR:]
    me = me_ref[0]
    rows = token_refs[0].shape[0]
    heads = weight_ref.shape[1] // (3 * HEAD)
    for k, ref in enumerate(token_refs):
        unit, _ = normalize(ref[...].astype(F32))
        norm = (unit * gain_ref[...] + shift_ref[...]).astype(BF)
        norm_ref[k * rows : (k + 1) * rows, :] = norm
        made_qkv = dot(norm, weight_ref[...]) + bias_ref[...]
        held[spot_of(k, me, rows), :] = made_qkv.astype(BF)
    for block in range(TENSOR):
        width = (block + 1) * rows
        distance = masked_distance(start_ref, block, rows)
        for head in range(heads):
            at = head * 3 * HEAD
            query = held[block * rows : width, at : at + HEAD]
            key = held[:width, at + HEAD : at + 2 * HEAD]
            value = held[:width, at + 2 * HEAD : at + 3 * HEAD]
            scores = dot(query, key, 1, 1) * SCALE - slope_ref[head] * distance
            best = jnp.max(scores, axis=1, keepdims=True)
            weights = jnp.exp(scores - best)
            mass = jnp.sum(weights, axis=1, keepdims=True)
            out = dot(weights.astype(BF), value) / mass
            made[block * rows : width, head * HEAD : (head + 1) * HEAD] = out.astype(BF)
            lse_ref[block * rows : width, head : head + 1] = best + jnp.log(mass)
    for k in range(TENSOR):
        part = made[spot_of(k, me, rows), :]
        ctx_refs[k][...] = part
        full_ref[k * rows : (k + 1) * rows, :] = part


def backward_kernel(first, me_ref, slope_ref, start_ref, lse_ref, held, *refs):
    outer_refs, (grad_ref, outer, keys, values, made) = refs[:TENSOR], refs[TENSOR:]
    me = me_ref[0]
    rows = held.shape[0] // TENSOR
    heads = made.shape[1] // (3 * HEAD)
    for k in range(TENSOR):
        outer[spot_of(k, me, rows), :] = outer_refs[k][...]
    for block in reversed(range(TENSOR)):
        width = (block + 1) * rows
        distance = masked_distance(start_ref, block, rows)
        for head in range(heads):
            at = head * 3 * HEAD
            cols = slice(head * HEAD, (head + 1) * HEAD)
            own = first + head
            took = own * 3 * HEAD
            query = held[block * rows : width, took : took + HEAD]
            key = held[:width, took + HEAD : took + 2 * HEAD]
            value = held[:width, took + 2 * HEAD : took + 3 * HEAD]
            grad = outer[block * rows : width, own * HEAD : (own + 1) * HEAD]
            lse = lse_ref[block * rows : width, own : own + 1]
            scores = dot(query, key, 1, 1) * SCALE - slope_ref[own] * distance
            probs = jnp.exp(scores - lse)
            prob_grad = dot(grad, value, 1, 1)
            delta = jnp.sum(probs * prob_grad, axis=1, keepdims=True)
            score_grad = (probs * (prob_grad - delta)).astype(BF)
            key_part = dot(score_grad, query, 0, 0)
            value_part = dot(probs.astype(BF), grad, 0, 0)
            if block == TENSOR - 1:
                keys[:width, cols] = key_part
                values[:width, cols] = value_part
            else:
                keys[:width, cols] += key_part
                values[:width, cols] += value_part
            made[block * rows : width, at : at + HEAD] = (dot(score_grad, key) * SCALE).astype(BF)
    for head in range(heads):
        at = head * 3 * HEAD
        cols = slice(head * HEAD, (head + 1) * HEAD)
        made[:, at + HEAD : at + 2 * HEAD] = (keys[:, cols] * SCALE).astype(BF)
        made[:, at + 2 * HEAD : at + 3 * HEAD] = values[:, cols].astype(BF)
    for k in range(TENSOR):
        grad_ref[k * rows : (k + 1) * rows, :] = made[spot_of(k, me, rows), :]


def attention(me, slopes, start, weight, bias, gain, shift, tokens):
    rows, model = tokens[0].shape
    width = weight.shape[1]
    total = rows * TENSOR
    wide = width // 3
    out = run(
        "attention_forward",
        forward_kernel,
        [((rows, wide), BF)] * TENSOR
        + [
            ((total, wide), BF),
            ((total, wide // HEAD), F32),
            ((total, width), BF),
            ((total, model), BF),
        ],
        [me, slopes],
        [start, weight, bias[None], gain[None], shift[None], *tokens],
        22,
        far=(1, 5, 6, 7, 8),
        scratch=[pltpu.VMEM((total, wide), BF)],
    )
    return out[:TENSOR], *out[TENSOR:]


def attention_back(me, slopes, start, lse, held, outer, first, heads):
    total, width = held.shape
    made = heads * 3 * HEAD
    return run(
        "attention_backward",
        functools.partial(backward_kernel, first),
        [((total, made), BF)],
        [me, slopes],
        [start, lse, held, *outer],
        28,
        far=(2, 3, 4, 5, 6),
        scratch=[
            pltpu.VMEM((total, width // 3), BF),
            pltpu.VMEM((total, heads * HEAD), F32),
            pltpu.VMEM((total, heads * HEAD), F32),
            pltpu.VMEM((total, made), BF),
        ],
    )[0]


def norm2_back_kernel(
    part_ref, beside_ref, across_ref, unit_ref, inverse_ref, gain_ref, cot_ref, *refs
):
    weight_refs, (resid_ref, low_ref, sums_ref), ctx_refs = (
        refs[:TENSOR],
        refs[TENSOR : TENSOR + 3],
        refs[TENSOR + 3 :],
    )
    rows = beside_ref.shape[0]
    grad = (
        part_ref[:rows, :].astype(F32)
        + beside_ref[...].astype(F32)
        + across_ref[...].astype(F32)
    )
    unit = unit_ref[...]
    resid = cot_ref[...].astype(F32) + norm_back(grad, unit, inverse_ref[...], gain_ref[...])
    low = resid.astype(BF)
    resid_ref[...] = resid
    low_ref[...] = low
    sums_ref[0:1, :] = jnp.sum(grad * unit, axis=0, keepdims=True)
    sums_ref[1:2, :] = jnp.sum(grad, axis=0, keepdims=True)
    sums_ref[2:3, :] = jnp.sum(low.astype(F32), axis=0, keepdims=True)
    sums_ref[3:4, :] = jnp.sum(cot_ref[...].astype(F32), axis=0, keepdims=True)
    for ctx, weight in zip(ctx_refs, weight_refs):
        ctx[...] = dot(low, weight[...], 1, 1).astype(BF)


def norm2_back(part, beside, across, unit, inverse, gain, cot, weights):
    rows, width = beside.shape
    out = run(
        "norm2_back",
        norm2_back_kernel,
        [((rows, width), F32), ((rows, width), BF), ((4, width), F32)]
        + [((rows, weight.shape[0]), BF) for weight in weights],
        [],
        [part, beside, across, unit, inverse, gain[None], cot, *weights],
        10,
        far=(1, 2, 6, 7, 8, 9, 10),
    )
    return out[0], out[1], out[2], out[3:]


def norm1_part_kernel(first_ref, second_ref, weight_ref, *refs):
    token_refs, part_refs, sums_ref = refs[:TENSOR], refs[TENSOR:-1], refs[-1]
    rows = token_refs[0].shape[0]
    cut = first_ref.shape[1]
    gain_sum, shift_sum = 0.0, 0.0
    for k, (tokens, part) in enumerate(zip(token_refs, part_refs)):
        spot = slice(k * rows, (k + 1) * rows)
        grad = dot(first_ref[spot, :], weight_ref[:, :cut], 1, 1)
        grad += dot(second_ref[spot, :], weight_ref[:, cut:], 1, 1)
        part[...] = grad.astype(BF)
        unit, _ = normalize(tokens[...].astype(F32))
        gain_sum += jnp.sum(grad * unit, axis=0, keepdims=True)
        shift_sum += jnp.sum(grad, axis=0, keepdims=True)
    sums_ref[0:1, :] = gain_sum
    sums_ref[1:2, :] = shift_sum


def norm1_back_kernel(*refs):
    part_refs, (tokens_ref, gain_ref, resid_ref, grad_ref) = refs[:TENSOR], refs[TENSOR:]
    grad = part_refs[0][...].astype(F32)
    for ref in part_refs[1:]:
        grad += ref[...].astype(F32)
    unit, inverse = normalize(tokens_ref[...].astype(F32))
    grad_ref[...] = (
        resid_ref[...] + norm_back(grad, unit, inverse, gain_ref[...])
    ).astype(BF)


def norm1_back(parts, tokens, gain, resid):
    return run(
        "norm1_back",
        norm1_back_kernel,
        [(tokens.shape, BF)],
        [],
        [*parts, tokens, gain[None], resid],
        12,
        far=(0, 1, 2, 3, 4, 6),
    )[0]


def dense_kernel(tokens_ref, bias_ref, gain_ref, shift_ref, *refs):
    heads_refs, refs = refs[:TENSOR], refs[TENSOR:]
    weight_refs, (resid_ref, norm_ref, unit_ref, inverse_ref) = refs[:TENSOR], refs[TENSOR:]
    total = dot(heads_refs[0][...], weight_refs[0][...])
    for k in range(1, TENSOR):
        total += dot(heads_refs[k][...], weight_refs[k][...])
    resid = tokens_ref[...].astype(F32) + (total + bias_ref[...])
    unit, inverse = normalize(resid)
    resid_ref[...] = resid
    unit_ref[...] = unit
    inverse_ref[...] = inverse
    norm_ref[...] = (unit * gain_ref[...] + shift_ref[...]).astype(BF)


def dense_norm(tokens, bias, gain, shift, mixed, weights):
    rows, width = tokens.shape
    return run(
        "dense_norm",
        dense_kernel,
        [((rows, width), F32), ((rows, width), BF), ((rows, width), F32), ((rows, 1), F32)],
        [],
        [tokens, bias[None], gain[None], shift[None], *mixed, *weights],
        10,
        far=(0, 4, 5, 6, 7, 8, 9, 10, 11),
    )


ROOT = math.sqrt(2.0 / math.pi)
CUBE = 0.044715


def feed_kernel(first_ref, second_ref, weight_ref, bias_ref, grad_ref, act_ref, pre_ref):
    rows = first_ref.shape[0]
    wide = min(256, weight_ref.shape[1])
    for i, ref in enumerate((first_ref, second_ref)):
        part = slice(i * rows, (i + 1) * rows)
        for at in range(0, weight_ref.shape[1], wide):
            cols = slice(at, at + wide)
            u = dot(ref[...], weight_ref[:, cols]) + bias_ref[:, cols]
            square = u * u
            bent = jnp.tanh(ROOT * (u + CUBE * (square * u)))
            half = 0.5 * (1.0 + bent)
            act_ref[part, cols] = (u * half).astype(BF)
            slope = half + 0.5 * u * (1.0 - bent * bent) * (ROOT + (3.0 * CUBE * ROOT) * square)
            pre_ref[part, cols] = (grad_ref[part, cols] * slope).astype(BF)


def feed(first, second, weight, bias, act_grad):
    shape = (2 * first.shape[0], weight.shape[1])
    return run(
        "feed_forward",
        feed_kernel,
        [(shape, BF)] * 2,
        [],
        [first, second, weight, bias[None], act_grad],
        12,
        far=(0, 1, 2),
    )


def rows_kernel(first_ref, second_ref, weight_ref, out_ref):
    rows = first_ref.shape[0]
    out_ref[:rows, :] = dot(first_ref[...], weight_ref[...], 1, 1)
    out_ref[rows:, :] = dot(second_ref[...], weight_ref[...], 1, 1)


def act_gradient(first, second, weight):
    shape = (2 * first.shape[0], weight.shape[0])
    return run("act_grad", rows_kernel, [(shape, F32)], [], [first, second, weight], 8)[0]


def part_kernel(side, value_ref, weight_ref, keep_ref, send_ref):
    rows = keep_ref.shape[0]
    keep_ref[...] = dot(value_ref[:rows, :], weight_ref[...], 1, side).astype(BF)
    send_ref[...] = dot(value_ref[rows:, :], weight_ref[...], 1, side).astype(BF)


def partial_rows(name, value, weight, side):
    shape = (value.shape[0] // 2, weight.shape[1 - side])
    body = functools.partial(part_kernel, side)
    return run(name, body, [(shape, BF)] * 2, [], [value, weight], 8)


def row_chunks(refs, rows):
    out = []
    for ref in refs:
        for at in range(0, ref.shape[0], rows):
            out.append((ref, slice(at, at + rows)))
    return out


def gradient_kernel(pieces, n_left, n_right, n_base, sums, places_ref, *refs):
    left, refs = refs[:n_left], refs[n_left:]
    right, refs = refs[:n_right], refs[n_right:]
    base, refs = refs[:n_base], refs[n_base:]
    rows = min(ref.shape[0] for ref in left + right)
    left = row_chunks(left, rows)
    right = row_chunks(right, rows)
    if pieces is None:
        height = refs[0].shape[0]
        pieces = [(0, height, None)]
    out = 0
    for first, height, bit in pieces:
        half = height if bit is None else height // 2
        step = min(256, half)
        for place in (None,) if bit is None else (1 - places_ref[bit], places_ref[bit]):
            for at in range(0, half, step):
                if place is None:
                    spot = pl.ds(first + at, step)
                else:
                    spot = pl.ds(pl.multiple_of(first + place * half + at, step), step)
                total = base[0][spot, :] if base else None
                for (l_ref, l_rows), (r_ref, r_rows) in zip(left, right):
                    term = dot(l_ref[l_rows, spot], r_ref[r_rows, :], 0, 0)
                    total = term if total is None else total + term
                refs[out][at : at + step, :] = total.astype(refs[out].dtype)
            out += 1
    if sums:
        total = None
        for ref, part in right:
            term = jnp.sum(ref[part, :].astype(F32), axis=0, keepdims=True)
            total = term if total is None else total + term
        refs[out][...] = total


def gradient(name, places, left, right, pieces, base=(), sums=False, mib=12):
    height, cols = left[0].shape[1], right[0].shape[1]
    if pieces is None:
        outs = [((height, cols), F32)]
    else:
        outs = [((rows // 2, cols), BF) for _, rows, _ in pieces for _ in range(2)]
    if sums:
        outs.append(((1, cols), F32))
    body = functools.partial(
        gradient_kernel, pieces, len(left), len(right), len(base), sums
    )
    return run(name, body, outs, [places], [*left, *right, *base], mib)


def output_kernel(resid_ref, bias_ref, *refs):
    mixed = refs[0][...].astype(F32)
    for ref in refs[1:-1]:
        mixed += ref[...].astype(F32)
    refs[-1][...] = (resid_ref[...] + (mixed + bias_ref[...])).astype(BF)


TAIL = 64


def late_kernel(bit, places_ref, norm_ref, first_ref, second_ref, context_ref, small_ref, *refs):
    resid_refs, (send_ref, keep_ref) = refs[:TENSOR], refs[TENSOR:]
    rows = resid_refs[0].shape[0]
    half = send_ref.shape[0] - TAIL
    cut = first_ref.shape[1]
    step = min(256, half)
    for out, place in ((send_ref, 1 - places_ref[bit]), (keep_ref, places_ref[bit])):
        for at in range(0, half, step):
            spot = pl.ds(pl.multiple_of(place * half + at, step), step)
            norm = norm_ref[:, spot]
            out[at : at + step, :cut] = dot(norm, first_ref[...], 0, 0).astype(BF)
            out[at : at + step, cut : 2 * cut] = dot(norm, second_ref[...], 0, 0).astype(BF)
            total = None
            for k, resid in enumerate(resid_refs):
                term = dot(resid[:, spot], context_ref[k * rows : (k + 1) * rows, :], 0, 0)
                total = term if total is None else total + term
            out[at : at + step, 2 * cut :] = total.astype(BF)
    width = send_ref.shape[1]
    last = jnp.concatenate(
        [
            jnp.sum(first_ref[...].astype(F32), axis=0, keepdims=True),
            jnp.sum(second_ref[...].astype(F32), axis=0, keepdims=True),
            jnp.zeros((1, width - 2 * cut), F32),
        ],
        axis=1,
    )
    count = small_ref.shape[0]
    tail = jnp.concatenate(
        [small_ref[...], last, jnp.zeros((TAIL - count - 1, width), F32)], axis=0
    ).astype(BF)
    send_ref[half:, :] = tail
    keep_ref[half:, :] = tail


def both_kernel(bit, places_ref, norm_ref, grad_ref, context_ref, small_ref, *refs):
    cut = grad_ref.shape[1] // 2
    first_ref, second_ref = grad_ref.at[:, :cut], grad_ref.at[:, cut:]
    resid_refs, refs = refs[:TENSOR], refs[TENSOR:]
    weight_ref, refs = refs[0], refs[1:]
    token_refs, refs = refs[:TENSOR], refs[TENSOR:]
    (send_ref, keep_ref), refs = refs[:2], refs[2:]
    part_refs, sums_ref = refs[:TENSOR], refs[TENSOR]
    norm1_part_kernel(
        first_ref, second_ref, weight_ref, *token_refs, *part_refs, sums_ref.at[0:2, :]
    )
    sums_ref[2:, :] = small_ref[...]
    late_kernel(
        bit, places_ref, norm_ref, first_ref, second_ref, context_ref, sums_ref, *resid_refs,
        send_ref, keep_ref,
    )


def late_gradient(places, bit, norm, grad, context, small, resid, weight, tokens):
    model = norm.shape[1]
    cols = grad.shape[1] + context.shape[1]
    shape = (model // 2 + TAIL, cols)
    return run(
        "qkv_dense",
        functools.partial(both_kernel, bit),
        [(shape, BF)] * 2 + [(tokens[0].shape, BF)] * TENSOR,
        [places],
        [norm, grad, context, small, *resid, weight, *tokens],
        22,
        far=(0, 2, 4, 5, 6, 7, 8, 9, 10, 11, 12),
        scratch=[pltpu.VMEM((2 + small.shape[0], model), F32)],
    )


def late_join_kernel(place_ref, mine_ref, got_ref, qkv_ref, dense_ref):
    rows = mine_ref.shape[0]
    cut = qkv_ref.shape[1]
    for ref, place in ((mine_ref, place_ref[0]), (got_ref, 1 - place_ref[0])):
        spot = pl.ds(pl.multiple_of(place * rows, rows), rows)
        qkv_ref[spot, :] = ref[:, :cut].astype(F32)
        dense_ref[:, spot] = ref[:, cut:].astype(F32).T


def unmix_kernel(place_ref, mine_ref, got_ref, late_ref, small_ref):
    rows = mine_ref.shape[0]
    rest = rows - TAIL

    def put(low_ref, high_ref):
        late_ref[:rows, :] = low_ref[...]
        late_ref[rows:, :] = high_ref[:rest, :]
        small_ref[...] = high_ref[rest:, :].astype(F32)

    @pl.when(place_ref[0] == 0)
    def _():
        put(mine_ref, got_ref)

    @pl.when(place_ref[0] != 0)
    def _():
        put(got_ref, mine_ref)


def unmix(place, mine, got):
    rows, cols = mine.shape
    return run(
        "qkv_dense_small_join",
        unmix_kernel,
        [((2 * rows - TAIL, cols), BF), ((TAIL, cols), F32)],
        [place],
        [mine, got],
    )


def late_join(cut, place, mine, got):
    rows, cols = mine.shape
    return run(
        "qkv_dense_join",
        late_join_kernel,
        [((2 * rows, cut), F32), ((cols - cut, 2 * rows), F32)],
        [place],
        [mine, got],
    )


def add_kernel(first_ref, second_ref, out_ref):
    out_ref[...] = (first_ref[...].astype(F32) + second_ref[...].astype(F32)).astype(BF)


def add_rows(first, second):
    return run("add_rows", add_kernel, [(first.shape, BF)], [], [first, second])[0]


def per_device(
    tokens,
    cotangent,
    seq_lengths,
    ln1_gain,
    ln1_bias,
    qkv_weight,
    qv_bias,
    dense_weight,
    dense_bias,
    ln2_gain,
    ln2_bias,
    up_weight,
    up_bias,
    down_weight,
    down_bias,
):
    rows = tokens.shape[0]
    total = rows * TENSOR
    heads = qkv_weight.shape[1] // (3 * HEAD)
    wide = heads * HEAD
    bits = dp_bits()
    x_first = list(range(bits))
    mixed_order = x_first[1::-1] + x_first[2:]
    rank = lax.axis_index("tensor")
    me = rank.astype(jnp.int32).reshape(1)
    slopes = jnp.exp2(
        -8.0 * ((rank * heads + jnp.arange(heads, dtype=jnp.int32)).astype(F32) + 1.0) / H
    )
    ends = jnp.cumsum(seq_lengths[0])
    positions = jnp.arange(total, dtype=jnp.int32)
    start = jnp.max(
        jnp.where(ends[None, :] <= positions[:, None], ends[None, :], 0), axis=1, keepdims=True
    )
    gain1, shift1 = ln1_gain.astype(F32), ln1_bias.astype(F32)
    gain2, shift2 = ln2_gain.astype(F32), ln2_bias.astype(F32)

    places = jnp.stack([my_bit(bit) for bit in range(bits)]).astype(jnp.int32)
    shares = 1 << min(bits, 2)
    piece = dense_weight.shape[0] // shares
    low_index = (lax.axis_index("dp") & (shares - 1)).astype(jnp.int32)
    part = swap(lax.dynamic_slice_in_dim(dense_weight, low_index * piece, piece, 0), 2)
    tokens_2 = swap(tokens, 2)
    tokens_1 = swap(tokens, 1)
    pair = qv_bias.astype(F32).reshape(heads, 2, HEAD)
    bias_full = jnp.stack([pair[:, 0], jnp.zeros_like(pair[:, 0]), pair[:, 1]], axis=1).reshape(
        3 * wide
    )
    cot_1 = swap(cotangent, 1)
    dense_1 = swap(dense_weight, 1)
    tokens_2, tokens_1, cot_1, dense_1, part, start, bias_full, slopes = lax.optimization_barrier(
        (tokens_2, tokens_1, cot_1, dense_1, part, start, bias_full, slopes)
    )
    tokens_3 = swap(tokens_2, 1)
    cot_2 = swap(after(cotangent, tokens_2), 2)
    count = lax.axis_size("dp")
    shared_parts = [part] + [
        lax.ppermute(part, "dp", [(i, i ^ k) for i in range(count)]) for k in range(1, shares)
    ]
    all_tokens = (tokens, tokens_1, tokens_2, tokens_3)
    blocks, context, lse, held, norm1 = attention(
        me, slopes, start, qkv_weight, bias_full, gain1, shift1, all_tokens
    )
    mixed_3 = swap(blocks[3], 3)
    mixed_2 = swap(blocks[2], 2)
    mixed_1 = swap(blocks[1], 1)
    *shared_parts, cot_2, _ = lax.optimization_barrier((*shared_parts, cot_2, context))
    (dense_2,) = run(
        "dense_rows",
        place_kernel,
        [(dense_weight.shape, BF)],
        [low_index.reshape(1)],
        list(shared_parts),
    )
    dense_3 = swap(dense_2, 1)
    dense = [dense_weight, dense_1, dense_2, dense_3]
    cot_3 = swap(cot_2, 1)
    act_grad_a = act_gradient(after(cotangent, dense_2), cot_1, down_weight)
    mixed = lax.optimization_barrier((blocks[0], mixed_1, mixed_2, mixed_3, act_grad_a))[:TENSOR]
    resid, norm2_0, unit2, inverse2 = dense_norm(
        tokens, dense_bias.astype(F32), gain2, shift2, mixed, dense
    )

    norm2_2 = swap(norm2_0, 2)
    norm2_1 = swap(norm2_0, 1)
    up_shift = up_bias.astype(F32)
    act_a, pre_a = feed(norm2_0, norm2_1, up_weight, up_shift, act_grad_a)
    act_grad_b = act_gradient(after(cot_2, act_a), cot_3, down_weight)
    (down_a,) = gradient("down_a", places, [act_a], [cotangent, cot_1], None)
    norm2_2 = lax.optimization_barrier((norm2_2, act_grad_b, down_a))[0]
    norm2_3 = swap(norm2_2, 1)
    act_b, pre_b = feed(norm2_2, norm2_3, up_weight, up_shift, act_grad_b)

    units = down_weight.shape[0]
    down_send, down_keep = gradient(
        "down", places, [act_b], [cot_2, cot_3], [(0, units, x_first[0])], [down_a]
    )
    down_sum = DpSum("down", down_send, down_keep, x_first[:2], [])
    keep_b, send_b = partial_rows("norm2_part_b", after(pre_b, down_keep), up_weight, 1)
    beside_b = swap(send_b, 1)
    model = up_weight.shape[0]
    norms = [norm2_0, norm2_1, norm2_2, norm2_3]
    keep_a, send_a = partial_rows("norm2_part_a", after(pre_a, keep_b), up_weight, 1)
    across = add_rows(keep_b, after(beside_b, keep_a))
    up_send, up_keep, up_shift_grad = gradient(
        "up", places, norms, [pre_a, after(pre_b, across)], [(0, model, mixed_order[0])], sums=True
    )
    across = swap(across, 2)
    up_sum = DpSum("up", up_send, up_keep, mixed_order[:2], [])
    beside_a = swap(send_a, 1)
    across = after(across, up_keep)
    resid_grad, resid_low, sums2, ctx_grad = norm2_back(
        keep_a, beside_a, across, unit2, inverse2, gain2, cotangent, dense
    )

    outer_3 = swap(ctx_grad[3], 3)
    outer_2 = swap(ctx_grad[2], 2)
    outer_1 = swap(ctx_grad[1], 1)
    resid_1 = swap(resid_low, 1)
    out_keep_b, out_send_b = partial_rows("out_part_b", after(act_b, resid_low), down_weight, 0)
    out_keep_a, out_send_a = partial_rows("out_part_a", after(act_a, resid_low), down_weight, 0)
    outer = lax.optimization_barrier(
        (ctx_grad[0], outer_1, outer_2, outer_3, out_keep_a, out_keep_b)
    )[:TENSOR]
    last = down_sum.step(*outer)
    last = up_sum.step(last)
    outer = lax.optimization_barrier((*outer, last))[:TENSOR]
    resid_2 = swap(after(resid_low, *outer), 2)
    qkv_grad = attention_back(me, slopes, start, lse, held, outer, 0, heads)
    late_bits = x_first[2:]
    place = my_bit(late_bits[0]).astype(jnp.int32).reshape(1)
    down_got, up_got, _ = lax.optimization_barrier((down_sum.got, up_sum.got, qkv_grad))
    quarter = down_sum.keep.shape[0]
    pair_send, pair_keep = run(
        "pair_add",
        pair_kernel,
        [((quarter // 2, 2 * model), BF)] * 2,
        [place],
        [down_sum.keep, down_got, up_sum.keep, up_got],
    )
    pair_sum = DpSum("pair", pair_send, pair_keep, late_bits, late_bits[::-1], pair_join)
    qkv_grad, resid_2, _ = lax.optimization_barrier((qkv_grad, resid_2, pair_keep))
    resid_3 = swap(resid_2, 1)
    units = up_shift_grad.shape[1]
    up_rows = jnp.pad(up_shift_grad, ((0, 0), (0, -units % model))).reshape(-1, model)
    small = jnp.concatenate([sums2, up_rows], axis=0)
    late_send, late_keep, *parts = late_gradient(
        places, x_first[0], norm1, qkv_grad, context, small,
        [resid_low, resid_1, resid_2, resid_3], qkv_weight, all_tokens,
    )
    late_sum = DpSum("late", late_send, late_keep, x_first, x_first[:0:-1], unmix)
    last = pair_sum.step(late_keep)
    part_3 = swap(after(parts[3], last), 3)
    part_2 = swap(after(parts[2], last), 2)
    part_1 = swap(after(parts[1], last), 1)
    out_1 = swap(after(out_send_a, part_1), 1)

    last = late_sum.step(out_1)
    while pair_sum.plan:
        last = pair_sum.step(last)
    down_rest, up_rest = pair_sum.value
    down_sum = DpSum("down", down_rest, down_rest, [], x_first[1::-1])
    up_sum = DpSum("up", up_rest, up_rest, [], mixed_order[1::-1])
    last = late_sum.step(down_rest)
    parts = lax.optimization_barrier((parts[0], part_1, part_2, part_3, last))[:TENSOR]
    grad_tokens = norm1_back(parts, tokens, gain1, resid_grad)
    out_3 = swap(after(out_send_b, grad_tokens), 3)
    out_2 = swap(after(out_keep_b, grad_tokens), 2)

    last = up_sum.step(grad_tokens)
    for _ in range(bits - 2):
        last = late_sum.step(last)
    last = down_sum.step(last)
    mixed = lax.optimization_barrier((out_keep_a, out_1, out_2, out_3, last))[:TENSOR]
    (output,) = run(
        "output",
        output_kernel,
        [(resid.shape, BF)],
        [],
        [resid, down_bias.astype(F32)[None], *mixed],
        12,
        far=(0, 2, 3, 4, 5),
    )
    last = late_sum.step(output)
    last = down_sum.step(last)
    while late_sum.plan:
        last = late_sum.step(last)
    late_rest, small = late_sum.value
    late_sum = DpSum(
        "late", late_rest, late_rest, [], x_first[:1], functools.partial(late_join, 3 * wide)
    )
    shared = small[:6]
    shared = shared + swap(shared, 1)
    shared = shared + swap(shared, 2)
    last = up_sum.step(shared)
    late_sum.step(last)
    count = up_rows.shape[0]
    up_total = small[6 : 6 + count].reshape(-1)[:units]
    slot_sums = small[6 + count, : 3 * wide].reshape(heads, 3, HEAD)
    grad_qv_bias = jnp.stack([slot_sums[:, 0], slot_sums[:, 2]], axis=1).reshape(2 * wide)
    return (
        output,
        grad_tokens,
        shared[0],
        shared[1],
        late_sum.value[0],
        grad_qv_bias,
        late_sum.value[1],
        shared[4],
        shared[2],
        shared[3],
        up_sum.value,
        up_total,
        down_sum.value,
        shared[5],
    )


def solution(mesh):
    return jax.shard_map(
        per_device,
        mesh=mesh,
        in_specs=(
            P(("dp", "tensor"), None),
            P(("dp", "tensor"), None),
            P("dp", None),
            P(),
            P(),
            P(None, "tensor"),
            P("tensor"),
            P("tensor", None),
            P(),
            P(),
            P(),
            P(None, "tensor"),
            P("tensor"),
            P("tensor", None),
            P(),
        ),
        out_specs=(
            P(("dp", "tensor"), None),
            P(("dp", "tensor"), None),
            P(),
            P(),
            P(None, "tensor"),
            P("tensor"),
            P("tensor", None),
            P(),
            P(),
            P(),
            P(None, "tensor"),
            P("tensor"),
            P("tensor", None),
            P(),
        ),
        check_vma=False,
    )
```
